256 devices in a mesh: dp: 32 (over x, z_hi, core), tensor: 8 (over y, z_lo).
Axes of the slice: x: 4, y: 4, z: 8 (z_hi: 4, z_lo: 2; z = z_hi * 2 + z_lo), core: 2. Of those that a mesh axis runs over, the one named last changes fastest.
Arguments:
- inputs: bfloat16 [20480, 4096], P(('dp', 'tensor')), may hold values from -8 to 8
- projections: bfloat16 [3, 4096, 2048], P(None, 'dp', 'tensor'), may hold values from -0.0625 to 0.0625
- upstream_grad: bfloat16 [20480, 2048], P('dp', 'tensor'), may hold values from -6 to 6
Outputs:
- input_grad: bfloat16 [20480, 4096], P(('dp', 'tensor'))
- weight_grad: float32 [3, 4096, 2048], P(None, 'dp', 'tensor')
The draws below stay inside these ranges and needn't reach their ends.
All inputs are finite; a program needn't handle non-finite values.
Results may differ from the reference program's by a relative error of at most 0.035.
Values may be sent and summed in bfloat16 or wider, within the bound.
A program may use at most 64 MiB of HBM per device.

```python
import jax
import jax.numpy as jnp
from jax import lax

D = 4096
HS = 128
SEQ = 640
HW = 2048
TOKENS = 20480
N_DP = 32
N_TENSOR = 8


def draw_inputs(key, part):
    key = jax.random.fold_in(key, 3)
    return jnp.clip(jax.random.normal(key, (TOKENS, D), jnp.float32), -6.0, 6.0).astype(jnp.bfloat16)


def draw_projections(key, part):
    key = jax.random.fold_in(key, 5)
    return (jnp.clip(jax.random.normal(key, (3, D, HW), jnp.float32), -4.0, 4.0) * D ** (-0.5)).astype(jnp.bfloat16)


def block_levels(rng, shape, shards, low, largest):
    level = 1.0
    for dim, parts in shards:
        steps = jax.random.uniform(jax.random.fold_in(jax.random.fold_in(rng, 6), dim), (parts,), jnp.float32, low / len(shards), largest / len(shards))
        level = level * jnp.repeat(jnp.exp(steps), shape[dim] // parts).reshape((-1,) + (1,) * (len(shape) - 1 - dim))
    return level


def centred(own_key, shape, width, bound, pieces=(), held_as=jnp.bfloat16):
    loudness = block_levels(own_key, shape, pieces, -0.22, 0.18) if pieces else 1.0
    values = jax.random.normal(own_key, shape, jnp.float32) * width * loudness
    return jnp.minimum(jnp.maximum(values, -bound), bound).astype(held_as)


def setup_inputs(seed: int = 0) -> dict:
    splits = jax.random.split(jax.random.key(seed), 4)
    inputs = draw_inputs(jax.random.fold_in(splits[3], 71), 0)
    projections = draw_projections(jax.random.fold_in(splits[3], 71), 0)
    upstream_grad = centred(splits[2], (TOKENS, HW), 1.0, 6.0, ((0, 32), (1, 8)))
    return dict(inputs=inputs, projections=projections, upstream_grad=upstream_grad)


def rotate(field, sign):
    half_size = HS // 2
    position = jnp.arange(field.shape[0], dtype=jnp.float32)
    frequency = 10000.0 ** (-jnp.arange(half_size, dtype=jnp.float32) / half_size)
    angles = position[:, None] * frequency[None, :]
    cosine = jnp.cos(angles)[:, None, :]
    sine_part = jnp.sin(angles)[:, None, :]
    first = field[..., :half_size]
    second = field[..., half_size:]
    return jnp.concatenate([first * cosine - sign * second * sine_part, second * cosine + sign * first * sine_part], -1)


def attend(projected, grad_out):
    length = projected.shape[1]
    heads_here = projected.shape[2] // HS
    score_scale = HS ** -0.5
    f32 = jnp.float32
    queries = rotate(projected[0].reshape(length, heads_here, HS), 1.0).astype(jnp.bfloat16)
    keys_rot = rotate(projected[1].reshape(length, heads_here, HS), 1.0).astype(jnp.bfloat16)
    values = projected[2].reshape(length, heads_here, HS).astype(jnp.bfloat16)
    scores = jnp.einsum("shd,thd->hst", queries.astype(f32), keys_rot.astype(f32)) * score_scale
    causal = jnp.arange(length)[:, None] >= jnp.arange(length)[None, :]
    scores = jnp.where(causal[None], scores, -1e30)
    raised = jnp.exp(scores - jnp.max(scores, -1, keepdims=True))
    probability = raised / jnp.sum(raised, -1, keepdims=True)
    probability_low = probability.astype(jnp.bfloat16)
    attended = jnp.einsum("hst,thd->shd", probability_low.astype(f32), values.astype(f32))
    upstream = grad_out.reshape(length, heads_here, HS)
    grad_values = jnp.einsum("hst,shd->thd", probability_low.astype(f32), upstream.astype(f32)).astype(jnp.bfloat16)
    grad_probs = jnp.einsum("shd,thd->hst", upstream.astype(f32), values.astype(f32))
    row_dots = jnp.transpose(jnp.sum(upstream.astype(f32) * attended, -1))
    grad_scores = (probability * (grad_probs - row_dots[:, :, None]) * score_scale).astype(jnp.bfloat16)
    grad_queries = jnp.einsum("hst,thd->shd", grad_scores.astype(f32), keys_rot.astype(f32))
    grad_keys = jnp.einsum("hst,shd->thd", grad_scores.astype(f32), queries.astype(f32))
    grad_queries = rotate(grad_queries, -1.0).astype(jnp.bfloat16)
    grad_keys = rotate(grad_keys, -1.0).astype(jnp.bfloat16)
    return jnp.stack([grad_queries, grad_keys, grad_values]).reshape(3, length, heads_here * HS)


def reference(inputs, projections, upstream_grad):
    f32 = jnp.float32
    sequences = inputs.reshape(N_DP, SEQ, D)
    upstreams = upstream_grad.reshape(N_DP, SEQ, HW)
    group_width = HW // N_TENSOR
    weights_full = projections.astype(f32)
    weight_groups = weights_full.reshape(3, D, N_TENSOR, group_width)

    def per_sequence(carry, item):
        local_x, local_up = item
        projected = jnp.einsum("sd,jdh->jsh", local_x.astype(f32), weights_full)
        grads = attend(projected, local_up)
        grouped = grads.astype(f32).reshape(3, SEQ, N_TENSOR, group_width)
        x_terms = jnp.einsum("jsgh,jdgh->gsd", grouped, weight_groups).astype(jnp.bfloat16)
        x_grad = jnp.sum(x_terms.astype(f32), 0).astype(jnp.bfloat16)
        w_term = jnp.einsum("sd,jsh->jdh", local_x.astype(f32), grads.astype(f32)).astype(jnp.bfloat16)
        return carry + w_term.astype(f32), x_grad

    total, x_grads = lax.scan(per_sequence, jnp.zeros((3, D, HW), jnp.float32), (sequences, upstreams))
    return x_grads.reshape(TOKENS, D), total
```

```python
import functools

import jax
import jax.numpy as jnp
import numpy as np
from jax import lax
from jax.experimental import pallas as pl
from jax.experimental.pallas import tpu as pltpu
from jax.sharding import PartitionSpec as P

HS = 128
SEQ = 640
D = 4096
MESH = pl.DeviceIdType.MESH
F32 = jnp.float32
BF16 = jnp.bfloat16
HALF = D // 2


def rotary_tables():
    half = HS // 2
    frequency = 10000.0 ** (-np.arange(half, dtype=np.float64) / half)
    angles = np.arange(SEQ, dtype=np.float64)[:, None] * frequency[None, :]
    cosine, sine = np.cos(angles), np.sin(angles)
    return (
        np.concatenate([cosine, cosine], -1).astype(np.float32),
        np.concatenate([-sine, sine], -1).astype(np.float32),
    )


def dot_nn(a, b):
    return lax.dot_general(a, b, (((1,), (0,)), ((), ())), preferred_element_type=F32)


def dot_nt(a, b):
    return lax.dot_general(a, b, (((1,), (1,)), ((), ())), preferred_element_type=F32)


def dot_tn(a, b):
    return lax.dot_general(a, b, (((0,), (0,)), ((), ())), preferred_element_type=F32)


N_SEND = 64
N_RECV = 64


def kernel(
    x_in, w_in, up_in, cos_in, sin_in, dx_out, dw_out,
    xv, wv, upv, cosv, sinv, qkv, gv, accv, dxp, dwp,
    rel_v, fin_v, zl_v, sib_v, xrel_v, xfin_v, zrel_v, zfin_v,
    send_sem, recv_sem, local_sem,
):
    dp = lax.axis_index("dp")
    tensor = lax.axis_index("tensor")
    x, zh, c = dp // 8, (dp // 2) % 4, dp % 2
    y, zl = tensor // 2, tensor % 2

    def place(xx, zz, cc, yy, ll):
        return {"dp": xx * 8 + zz * 2 + cc, "tensor": yy * 2 + ll}

    def ring(v, step):
        return lax.rem(v + (step + 4), 4)

    yp, ym = place(x, zh, c, ring(y, 1), zl), place(x, zh, c, ring(y, -1), zl)
    xp, xm = place(ring(x, 1), zh, c, y, zl), place(ring(x, -1), zh, c, y, zl)
    zp, zm = place(x, ring(zh, 1), c, y, zl), place(x, ring(zh, -1), c, y, zl)
    mate = place(x, zh, c, y, 1 - zl)
    sibling = place(x, zh, 1 - c, y, zl)
    everyone = (yp, ym, xp, xm, zp, zm, mate, sibling)

    keys = {}
    sends = []

    def key_index(key):
        return keys.setdefault(key, len(keys))

    def send(src, dst, key, device):
        copy = pltpu.make_async_remote_copy(
            src_ref=src, dst_ref=dst, send_sem=send_sem.at[len(sends)],
            recv_sem=recv_sem.at[key_index(key)], device_id=device, device_id_type=MESH,
        )
        copy.start()
        sends.append(copy)

    def recv(dst, key, device):
        pltpu.make_async_remote_copy(
            src_ref=dst, dst_ref=dst, send_sem=send_sem.at[0],
            recv_sem=recv_sem.at[key_index(key)], device_id=device, device_id_type=MESH,
        ).wait_recv()

    def rows(yy, ll):
        return pl.ds(pl.multiple_of(yy * 160 + ll * 80, 16), 80)

    def cols(h):
        return pl.ds(h * HALF, HALF)

    own_x = xv.at[rows(y, zl)]

    def unit(xx, zz):
        return wv.at[:, xx * 4 + zz, c]

    locals_ = [
        pltpu.make_async_copy(x_in, own_x, local_sem.at[0]),
        pltpu.make_async_copy(w_in, unit(x, zh), local_sem.at[1]),
        pltpu.make_async_copy(up_in, upv, local_sem.at[2]),
        pltpu.make_async_copy(cos_in, cosv, local_sem.at[3]),
        pltpu.make_async_copy(sin_in, sinv, local_sem.at[4]),
    ]
    for copy in locals_:
        copy.start()

    barrier = pltpu.get_barrier_semaphore()
    for device in everyone:
        pl.semaphore_signal(barrier, inc=1, device_id=device, device_id_type=MESH)
    pl.semaphore_wait(barrier, len(everyone))

    send(x_in, own_x, "Xp", mate)
    send(w_in, unit(x, zh), ("W", 0, -1), zp)
    send(w_in, unit(x, zh), ("W", 0, 1), zm)
    send(x_in, own_x, ("Xo", -1), yp)
    send(x_in, own_x, ("Xo", 1), ym)
    send(w_in, unit(x, zh), ("W", -1, 0), xp)
    send(w_in, unit(x, zh), ("W", 1, 0), xm)
    for copy in locals_:
        copy.wait()

    top, bottom = pl.ds(0, 64), pl.ds(64, 64)

    def unit_half(xx, zz, part):
        return wv.at[:, xx * 4 + zz, c, part]

    def group(xx, cc):
        return wv.at[:, pl.ds(xx * 4, 4), cc]

    xn, xq, x2 = ring(x, -1), ring(x, 1), ring(x, 2)
    zn, zq, z2 = ring(zh, -1), ring(zh, 1), ring(zh, 2)
    yn, yq, y2 = ring(y, -1), ring(y, 1), ring(y, 2)

    recv(unit(x, zn), ("W", 0, -1), zm)
    send(unit_half(x, zn, top), unit_half(x, zn, top), "WrA", zp)
    send(unit(x, zn), unit(x, zn), ("W", -1, -1), xp)
    send(unit(x, zn), unit(x, zn), ("W", 1, -1), xm)
    recv(unit(x, zq), ("W", 0, 1), zp)
    send(unit_half(x, zq, bottom), unit_half(x, zq, bottom), "WrB", zm)
    send(unit(x, zq), unit(x, zq), ("W", -1, 1), xp)
    send(unit(x, zq), unit(x, zq), ("W", 1, 1), xm)

    recv(unit(xn, zh), ("W", -1, 0), xm)
    send(unit(xn, zh), unit(xn, zh), ("W", 2, 0), xp)
    recv(unit(xq, zh), ("W", 1, 0), xp)

    own, other = rows(y, zl), rows(y, 1 - zl)
    recv(xv.at[other], "Xp", mate)
    send(xv.at[other], xv.at[other], ("Xq", -1), yp)
    send(xv.at[other], xv.at[other], ("Xq", 1), ym)
    blk = rows(yn, zl)
    recv(xv.at[blk], ("Xo", -1), ym)
    send(xv.at[blk, cols(0)], xv.at[blk, cols(0)], ("Xr", 0, 0), yp)
    blk = rows(yq, zl)
    recv(xv.at[blk], ("Xo", 1), yp)
    send(xv.at[blk, cols(1)], xv.at[blk, cols(1)], ("Xr", 0, 1), ym)

    recv(unit_half(x, z2, top), "WrA", zm)
    recv(unit_half(x, z2, bottom), "WrB", zp)
    send(unit(x, z2), unit(x, z2), ("W", -1, 2), xp)
    send(unit(x, z2), unit(x, z2), ("W", 1, 2), xm)
    send(group(x, c), group(x, c), ("S", 0), sibling)

    recv(unit(xn, zn), ("W", -1, -1), xm)
    send(unit(xn, zn), unit(xn, zn), ("W", 2, -1), xp)
    recv(unit(xq, zq), ("W", 1, 1), xp)
    send(unit(xq, zq), unit(xq, zq), ("W", 2, 1), xm)
    recv(unit(xq, zn), ("W", 1, -1), xp)
    recv(unit(xn, zq), ("W", -1, 1), xm)
    recv(unit(xq, z2), ("W", 1, 2), xp)
    send(unit(xq, z2), unit(xq, z2), ("W", 2, 2), xm)
    recv(unit(xn, z2), ("W", -1, 2), xm)
    send(group(xn, c), group(xn, c), ("S", -1), sibling)
    send(group(xq, c), group(xq, c), ("S", 1), sibling)

    blk = rows(yn, 1 - zl)
    recv(xv.at[blk], ("Xq", -1), ym)
    send(xv.at[blk, cols(0)], xv.at[blk, cols(0)], ("Xr", 1, 0), yp)
    blk = rows(yq, 1 - zl)
    recv(xv.at[blk], ("Xq", 1), yp)
    send(xv.at[blk, cols(1)], xv.at[blk, cols(1)], ("Xr", 1, 1), ym)

    recv(unit(x2, zh), ("W", 2, 0), xm)
    recv(unit(x2, zn), ("W", 2, -1), xm)
    recv(unit(x2, zq), ("W", 2, 1), xp)
    recv(unit(x2, z2), ("W", 2, 2), xp)
    send(group(x2, c), group(x2, c), ("S", 2), sibling)
    recv(group(x, 1 - c), ("S", 0), sibling)
    recv(group(xn, 1 - c), ("S", -1), sibling)
    recv(group(xq, 1 - c), ("S", 1), sibling)
    recv(group(x2, 1 - c), ("S", 2), sibling)

    def project(yy):
        r = pl.ds(pl.multiple_of(yy * 160, 32), 160)
        cosine, sine = cosv[r], sinv[r]

        @pl.loop(0, 3)
        def _(j):
            p = dot_nn(xv[r], wv[j].reshape(D, 256))
            rotated = j < 2
            cc = jnp.where(rotated, cosine, 1.0)
            ss = jnp.where(rotated, sine, 0.0)
            for h in range(2):
                ph = p[:, h * HS:(h + 1) * HS]
                qkv[j, h, r] = (ph * cc + pltpu.roll(ph, 64, 1) * ss).astype(BF16)

    project(y)
    project(yn)
    project(yq)
    recv(xv.at[rows(y2, zl), cols(0)], ("Xr", 0, 0), ym)
    recv(xv.at[rows(y2, zl), cols(1)], ("Xr", 0, 1), yp)
    recv(xv.at[rows(y2, 1 - zl), cols(0)], ("Xr", 1, 0), ym)
    recv(xv.at[rows(y2, 1 - zl), cols(1)], ("Xr", 1, 1), yp)
    project(y2)

    scale = HS ** -0.5
    lower = lax.broadcasted_iota(jnp.int32, (128, 128), 0) >= lax.broadcasted_iota(
        jnp.int32, (128, 128), 1
    )

    def rotate_back(v, r):
        return (v * cosv[r] - pltpu.roll(v, 64, 1) * sinv[r]).astype(BF16)

    for h in range(2):
        hc = pl.ds(h * HS, HS)
        for i in reversed(range(5)):
            n = (i + 1) * 128
            r = pl.ds(i * 128, 128)
            head = pl.ds(0, n)
            q, k, v = qkv[0, h, r], qkv[1, h, head], qkv[2, h, head]
            up = upv[r, hc]
            s = dot_nt(q, k) * scale
            diagonal = jnp.where(lower, s[:, i * 128:], -1e30)
            s = diagonal if i == 0 else jnp.concatenate([s[:, : i * 128], diagonal], 1)
            e = jnp.exp(s - jnp.max(s, 1, keepdims=True))
            prob = e / jnp.sum(e, 1, keepdims=True)
            low = prob.astype(BF16)
            gp = dot_nt(up, v)
            att = dot_nn(low, v)
            dots = jnp.sum(up.astype(F32) * att, 1, keepdims=True)
            gs = (prob * (gp - dots) * scale).astype(BF16)
            gv[r, pl.ds(h * HS, HS)] = rotate_back(dot_nn(gs, k), r)
            dk, dv = dot_tn(gs, q), dot_tn(low, up)
            if i == 4:
                accv[0], accv[1] = dk, dv
            else:
                accv[0, head] += dk
                accv[1, head] += dv
        full = pl.ds(0, SEQ)
        gv[:, pl.ds(256 + h * HS, HS)] = rotate_back(accv[0], full)
        gv[:, pl.ds(512 + h * HS, HS)] = accv[1].astype(BF16)

    def x_term(yy):
        r = pl.ds(pl.multiple_of(yy * 160, 32), 160)

        @pl.loop(0, 4)
        def _(i):
            total = None
            for j in range(3):
                w = wv[j, pl.ds(i * 4, 4)].reshape(1024, 256)
                t = dot_nt(gv[r, pl.ds(j * 256, 256)], w)
                total = t if total is None else total + t
            dxp[r, pl.ds(pl.multiple_of(i * 1024, 1024), 1024)] = total.astype(BF16)

    def w_term(xx):
        @pl.loop(0, 4)
        def _(i):
            b = xx * 4 + i
            t = dot_tn(xv[:, pl.ds(pl.multiple_of(b * 256, 256), 256)], gv[...])
            for cc in range(2):
                for j in range(3):
                    dwp[b, cc, j] = t[cc * 128:(cc + 1) * 128, j * 256:(j + 1) * 256].astype(BF16)

    def add_into(dst, src):
        dst[...] = (dst[...].astype(F32) + src[...].astype(F32)).astype(BF16)

    def xpart(yy, dz, h):
        return dxp.at[rows(yy, zl if dz == 0 else 1 - zl), cols(h)]

    def wgroup(xx, cc, first=0, count=4):
        return dwp.at[pl.ds(xx * 4 + first, count), cc]

    def send_sib(xx, dx):
        send(wgroup(xx, 1 - c), sib_v.at[pl.ds(xx * 4, 4)], ("DS", dx), sibling)

    def recv_sib(xx, dx):
        recv(sib_v.at[pl.ds(xx * 4, 4)], ("DS", dx), sibling)

        @pl.loop(0, 4)
        def _(i):
            add_into(dwp.at[xx * 4 + i, c], sib_v.at[xx * 4 + i])

    x_term(y2)
    for dz in (1, 0):
        send(xpart(y2, dz, 0), rel_v.at[0, dz], ("R", 0, dz), yp)
        send(xpart(y2, dz, 1), rel_v.at[1, dz], ("R", 1, dz), ym)
    w_term(x2)
    send_sib(x2, 2)
    x_term(yq)
    send(xpart(yq, 1, 1), fin_v.at[0, 1, 1], ("F", 0, 1, 1), yp)
    x_term(yn)
    send(xpart(yn, 1, 0), fin_v.at[1, 1, 0], ("F", 1, 1, 0), ym)
    recv_sib(x2, 2)
    send(wgroup(x2, c, 0, 2), xrel_v.at[0], ("XR", 0), xp)
    send(wgroup(x2, c, 2, 2), xrel_v.at[1], ("XR", 1), xm)
    w_term(xq)
    send_sib(xq, 1)
    w_term(xn)
    send_sib(xn, -1)
    for dz in (1, 0):
        if dz == 0:
            send(xpart(yq, 0, 1), fin_v.at[0, 0, 1], ("F", 0, 0, 1), yp)
            send(xpart(yn, 0, 0), fin_v.at[1, 0, 0], ("F", 1, 0, 0), ym)
        recv(rel_v.at[0, dz], ("R", 0, dz), ym)
        add_into(xpart(yq, dz, 0), rel_v.at[0, dz])
        send(xpart(yq, dz, 0), fin_v.at[0, dz, 0], ("F", 0, dz, 0), yp)
        recv(rel_v.at[1, dz], ("R", 1, dz), yp)
        add_into(xpart(yn, dz, 1), rel_v.at[1, dz])
        send(xpart(yn, dz, 1), fin_v.at[1, dz, 1], ("F", 1, dz, 1), ym)
    recv_sib(xq, 1)
    send(wgroup(xq, c, 2, 2), xfin_v.at[0, pl.ds(2, 2)], ("XF", 0, 2), xp)
    recv_sib(xn, -1)
    send(wgroup(xn, c, 0, 2), xfin_v.at[1, pl.ds(0, 2)], ("XF", 1, 0), xm)
    x_term(y)
    w_term(x)
    send_sib(x, 0)
    recv(xrel_v.at[0], ("XR", 0), xm)
    for i in range(2):
        add_into(dwp.at[xq * 4 + i, c], xrel_v.at[0, i])
    send(wgroup(xq, c, 0, 2), xfin_v.at[0, pl.ds(0, 2)], ("XF", 0, 0), xp)
    recv(xrel_v.at[1], ("XR", 1), xp)
    for i in range(2):
        add_into(dwp.at[xn * 4 + 2 + i, c], xrel_v.at[1, i])
    send(wgroup(xn, c, 2, 2), xfin_v.at[1, pl.ds(2, 2)], ("XF", 1, 2), xm)
    recv_sib(x, 0)

    for h in (1, 0):
        recv(fin_v.at[0, 1, h], ("F", 0, 1, h), ym)
        recv(fin_v.at[1, 1, h], ("F", 1, 1, h), yp)
        part = xpart(y, 1, h)
        part[...] = (
            part[...].astype(F32) + fin_v[0, 1, h].astype(F32) + fin_v[1, 1, h].astype(F32)
        ).astype(BF16)
        send(part, zl_v.at[h], ("Z", h), mate)

    for first in (2, 0):
        recv(xfin_v.at[0, pl.ds(first, 2)], ("XF", 0, first), xm)
    for first in (0, 2):
        recv(xfin_v.at[1, pl.ds(first, 2)], ("XF", 1, first), xp)

    @pl.loop(0, 4)
    def _(i):
        dst = dwp.at[x * 4 + i, c]
        dst[...] = (
            dst[...].astype(F32) + xfin_v[0, i].astype(F32) + xfin_v[1, i].astype(F32)
        ).astype(BF16)

    def wz(zz):
        return dwp.at[x * 4 + zz, c]

    def wz_half(zz, part):
        return dwp.at[x * 4 + zz, c, :, part]

    send(wz_half(z2, top), zrel_v.at[0], ("ZR", 0), zp)
    send(wz_half(z2, bottom), zrel_v.at[1], ("ZR", 1), zm)
    send(wz_half(zq, bottom), zfin_v.at[0, :, bottom], ("ZF", 0, 1), zp)
    send(wz_half(zn, top), zfin_v.at[1, :, top], ("ZF", 1, 0), zm)
    recv(zrel_v.at[0], ("ZR", 0), zm)
    add_into(wz_half(zq, top), zrel_v.at[0])
    send(wz_half(zq, top), zfin_v.at[0, :, top], ("ZF", 0, 0), zp)
    recv(zrel_v.at[1], ("ZR", 1), zp)
    add_into(wz_half(zn, bottom), zrel_v.at[1])
    send(wz_half(zn, bottom), zfin_v.at[1, :, bottom], ("ZF", 1, 1), zm)

    for h in (1, 0):
        recv(fin_v.at[0, 0, h], ("F", 0, 0, h), ym)
        recv(fin_v.at[1, 0, h], ("F", 1, 0, h), yp)
        recv(zl_v.at[h], ("Z", h), mate)
        dx_out[:, h * HALF:(h + 1) * HALF] = (
            xpart(y, 0, h)[...].astype(F32)
            + fin_v[0, 0, h].astype(F32)
            + fin_v[1, 0, h].astype(F32)
            + zl_v[h].astype(F32)
        ).astype(BF16)

    recv(zfin_v.at[0, :, bottom], ("ZF", 0, 1), zm)
    recv(zfin_v.at[0, :, top], ("ZF", 0, 0), zm)
    recv(zfin_v.at[1, :, top], ("ZF", 1, 0), zp)
    recv(zfin_v.at[1, :, bottom], ("ZF", 1, 1), zp)
    dw_out[...] = wz(zh)[...].astype(F32) + zfin_v[0].astype(F32) + zfin_v[1].astype(F32)

    for copy in sends:
        copy.wait_send()
    assert len(sends) <= N_SEND and len(keys) <= N_RECV


def shards(inputs, projections, upstream_grad):
    cosine, sine = rotary_tables()
    any_spec = pl.BlockSpec(memory_space=pl.ANY)
    vmem = pl.BlockSpec(memory_space=pltpu.VMEM)
    return pl.pallas_call(
        kernel,
        out_shape=(
            jax.ShapeDtypeStruct((80, D), BF16),
            jax.ShapeDtypeStruct((3, 128, 256), F32),
        ),
        in_specs=[any_spec] * 5,
        out_specs=(vmem, vmem),
        scratch_shapes=[
            pltpu.VMEM((SEQ, D), BF16),
            pltpu.VMEM((3, 16, 2, 128, 256), BF16),
            pltpu.VMEM((SEQ, 256), BF16),
            pltpu.VMEM((SEQ, HS), F32),
            pltpu.VMEM((SEQ, HS), F32),
            pltpu.VMEM((3, 2, SEQ, HS), BF16),
            pltpu.VMEM((SEQ, 768), BF16),
            pltpu.VMEM((2, SEQ, HS), F32),
            pltpu.VMEM((SEQ, D), BF16),
            pltpu.VMEM((16, 2, 3, 128, 256), BF16),
            pltpu.VMEM((2, 2, 80, HALF), BF16),
            pltpu.VMEM((2, 2, 2, 80, HALF), BF16),
            pltpu.VMEM((2, 80, HALF), BF16),
            pltpu.VMEM((16, 3, 128, 256), BF16),
            pltpu.VMEM((2, 2, 3, 128, 256), BF16),
            pltpu.VMEM((2, 4, 3, 128, 256), BF16),
            pltpu.VMEM((2, 3, 64, 256), BF16),
            pltpu.VMEM((2, 3, 128, 256), BF16),
            pltpu.SemaphoreType.DMA((N_SEND,)),
            pltpu.SemaphoreType.DMA((N_RECV,)),
            pltpu.SemaphoreType.DMA((5,)),
        ],
        compiler_params=pltpu.CompilerParams(
            collective_id=0, has_side_effects=True, vmem_limit_bytes=60 * 2**20
        ),
        name="mixer_backward",
    )(inputs, projections, upstream_grad, jnp.asarray(cosine), jnp.asarray(sine))


def solution(mesh):
    return jax.shard_map(
        shards,
        mesh=mesh,
        in_specs=(P(("dp", "tensor"), None), P(None, "dp", "tensor"), P("dp", "tensor")),
        out_specs=(P(("dp", "tensor"), None), P(None, "dp", "tensor")),
        check_vma=False,
    )
```

```python
import functools

import jax
import jax.numpy as jnp
import numpy as np
from jax import lax
from jax.experimental import pallas as pl
from jax.experimental.pallas import tpu as pltpu
from jax.sharding import PartitionSpec as P

HS = 128
SEQ = 640
D = 4096
MESH = pl.DeviceIdType.MESH
F32 = jnp.float32
BF16 = jnp.bfloat16
HALF = D // 2
POSITION = {2: 0, 1: 1, -1: 2, 0: 3}


def rotary_tables():
    half = HS // 2
    frequency = 10000.0 ** (-np.arange(half, dtype=np.float64) / half)
    angles = np.arange(SEQ, dtype=np.float64)[:, None] * frequency[None, :]
    cosine, sine = np.cos(angles), np.sin(angles)
    return (
        np.concatenate([cosine, cosine], -1).astype(np.float32),
        np.concatenate([-sine, sine], -1).astype(np.float32),
    )


def dot_nn(a, b):
    return lax.dot_general(a, b, (((1,), (0,)), ((), ())), preferred_element_type=F32)


def dot_nt(a, b):
    return lax.dot_general(a, b, (((1,), (1,)), ((), ())), preferred_element_type=F32)


def dot_tn(a, b):
    return lax.dot_general(a, b, (((0,), (0,)), ((), ())), preferred_element_type=F32)


N_SEND = 96
N_RECV = 96


def kernel(
    x_in, w_in, up_in, cos_in, sin_in, dx_out, dw_out,
    xv, wv, upv, cosv, sinv, pacc, qkv, gv, gr, accv, dxp, dwp,
    rel_v, fin_v, zl_v, sib_v, xrel_v, xfin_v, zrel_v, zfin_v,
    send_sem, recv_sem, local_sem,
):
    dp = lax.axis_index("dp")
    tensor = lax.axis_index("tensor")
    x, zh, c = dp // 8, (dp // 2) % 4, dp % 2
    y, zl = tensor // 2, tensor % 2

    def place(xx, zz, cc, yy, ll):
        return {"dp": xx * 8 + zz * 2 + cc, "tensor": yy * 2 + ll}

    def ring(v, step):
        return lax.rem(v + (step + 4), 4)

    yp, ym = place(x, zh, c, ring(y, 1), zl), place(x, zh, c, ring(y, -1), zl)
    xp, xm = place(ring(x, 1), zh, c, y, zl), place(ring(x, -1), zh, c, y, zl)
    zp, zm = place(x, ring(zh, 1), c, y, zl), place(x, ring(zh, -1), c, y, zl)
    mate = place(x, zh, c, y, 1 - zl)
    sibling = place(x, zh, 1 - c, y, zl)
    everyone = (yp, ym, xp, xm, zp, zm, mate, sibling)

    keys = {}
    sends = []

    def key_index(key):
        return keys.setdefault(key, len(keys))

    def send(src, dst, key, device):
        copy = pltpu.make_async_remote_copy(
            src_ref=src, dst_ref=dst, send_sem=send_sem.at[len(sends)],
            recv_sem=recv_sem.at[key_index(key)], device_id=device, device_id_type=MESH,
        )
        copy.start()
        sends.append(copy)

    def recv(dst, key, device):
        pltpu.make_async_remote_copy(
            src_ref=dst, dst_ref=dst, send_sem=send_sem.at[0],
            recv_sem=recv_sem.at[key_index(key)], device_id=device, device_id_type=MESH,
        ).wait_recv()

    def rows(yy, ll):
        return pl.ds(pl.multiple_of(yy * 160 + ll * 80, 16), 80)

    def cols(h):
        return pl.ds(h * HALF, HALF)

    def slot(dy, dz):
        return pl.ds(160 * POSITION[dy] + 80 * dz, 80)

    own_x = xv.at[slot(0, 0)]

    def unit(xx, zz):
        return wv.at[:, xx * 4 + zz, c]

    locals_ = [
        pltpu.make_async_copy(x_in, own_x, local_sem.at[0]),
        pltpu.make_async_copy(w_in, unit(x, zh), local_sem.at[1]),
        pltpu.make_async_copy(up_in, upv, local_sem.at[2]),
        pltpu.make_async_copy(cos_in, cosv, local_sem.at[3]),
        pltpu.make_async_copy(sin_in, sinv, local_sem.at[4]),
    ]
    for copy in locals_:
        copy.start()

    barrier = pltpu.get_barrier_semaphore()
    for device in everyone:
        pl.semaphore_signal(barrier, inc=1, device_id=device, device_id_type=MESH)
    pl.semaphore_wait(barrier, len(everyone))

    top, bottom = pl.ds(0, 64), pl.ds(64, 64)

    def unit_half(xx, zz, part):
        return wv.at[:, xx * 4 + zz, c, part]

    def group(xx, cc):
        return wv.at[:, pl.ds(xx * 4, 4), cc]

    xn, xq, x2 = ring(x, -1), ring(x, 1), ring(x, 2)
    zn, zq, z2 = ring(zh, -1), ring(zh, 1), ring(zh, 2)

    def quarter(k):
        return pl.ds(k * 1024, 1024)

    def xpiece(dy, dz, part):
        return xv.at[slot(dy, dz), part]

    def to_mate(k):
        send(x_in.at[:, quarter(k)], xpiece(0, 1, quarter(k)), ("Xp", k), mate)

    to_mate(0)
    to_mate(2)
    send(w_in, unit(x, zh), ("W", 0, -1), zp)
    send(w_in, unit(x, zh), ("W", 0, 1), zm)
    for h in range(2):
        send(x_in.at[:, cols(h)], xpiece(-1, 0, cols(h)), ("Xo", -1, h), yp)
        send(x_in.at[:, cols(1 - h)], xpiece(1, 0, cols(1 - h)), ("Xo", 1, 1 - h), ym)
    send(w_in, unit(x, zh), ("W", -1, 0), xp)
    send(w_in, unit(x, zh), ("W", 1, 0), xm)
    for copy in locals_:
        copy.wait()

    def pass_on(piece, key, device):
        send(piece, piece, key, device)

    def mate_piece(k):
        piece = xpiece(0, 1, quarter(k))
        recv(piece, ("Xp", k), mate)
        send(piece, xpiece(-1, 1, quarter(k)), ("Xq", -1, k), yp)
        send(piece, xpiece(1, 1, quarter(k)), ("Xq", 1, k), ym)

    def far_piece(k):
        dy, source, device = (-1, ym, yp) if k < 2 else (1, yp, ym)
        piece = xpiece(dy, 1, quarter(k))
        recv(piece, ("Xq", dy, k), source)
        send(piece, xpiece(2, 1, quarter(k)), ("Xr", 1, k), device)

    recv(unit(xn, zh), ("W", -1, 0), xm)
    pass_on(unit(xn, zh), ("W", 2, 0), xp)
    recv(unit(xq, zh), ("W", 1, 0), xp)

    mate_piece(0)
    mate_piece(2)
    to_mate(1)
    to_mate(3)
    recv(unit(x, zn), ("W", 0, -1), zm)
    pass_on(unit_half(x, zn, top), "WrA", zp)
    pass_on(unit(x, zn), ("W", -1, -1), xp)
    pass_on(unit(x, zn), ("W", 1, -1), xm)
    recv(unit(x, zq), ("W", 0, 1), zp)
    pass_on(unit_half(x, zq, bottom), "WrB", zm)
    pass_on(unit(x, zq), ("W", -1, 1), xp)
    pass_on(unit(x, zq), ("W", 1, 1), xm)

    recv(xpiece(-1, 0, cols(0)), ("Xo", -1, 0), ym)
    send(xpiece(-1, 0, cols(0)), xpiece(2, 0, cols(0)), ("Xr", 0, 0), yp)
    recv(xpiece(1, 0, cols(1)), ("Xo", 1, 1), yp)
    send(xpiece(1, 0, cols(1)), xpiece(2, 0, cols(1)), ("Xr", 0, 1), ym)

    recv(unit_half(x, z2, top), "WrA", zm)
    recv(unit_half(x, z2, bottom), "WrB", zp)
    pass_on(unit(x, z2), ("W", -1, 2), xp)
    pass_on(unit(x, z2), ("W", 1, 2), xm)
    pass_on(group(x, c), ("S", 0), sibling)
    mate_piece(1)
    mate_piece(3)

    recv(unit(xn, zn), ("W", -1, -1), xm)
    pass_on(unit(xn, zn), ("W", 2, -1), xp)
    recv(unit(xq, zq), ("W", 1, 1), xp)
    pass_on(unit(xq, zq), ("W", 2, 1), xm)
    far_piece(0)
    far_piece(2)
    recv(unit(xq, zn), ("W", 1, -1), xp)
    recv(unit(xn, zq), ("W", -1, 1), xm)
    recv(unit(xq, z2), ("W", 1, 2), xp)
    pass_on(unit(xq, z2), ("W", 2, 2), xm)
    recv(unit(xn, z2), ("W", -1, 2), xm)
    pass_on(group(xn, c), ("S", -1), sibling)
    pass_on(group(xq, c), ("S", 1), sibling)
    far_piece(1)
    far_piece(3)

    recv(xpiece(-1, 0, cols(1)), ("Xo", -1, 1), ym)
    recv(xpiece(1, 0, cols(0)), ("Xo", 1, 0), yp)
    for k in (2, 3):
        recv(xpiece(-1, 1, quarter(k)), ("Xq", -1, k), ym)
    for k in (0, 1):
        recv(xpiece(1, 1, quarter(k)), ("Xq", 1, k), yp)
    near_rows = pl.ds(160, 480)

    def project_group(xx, first):
        @pl.loop(0, 3)
        def _(j):
            t = dot_nn(
                xv[near_rows, pl.ds(pl.multiple_of(xx * 1024, 1024), 1024)],
                wv[j, pl.ds(xx * 4, 4)].reshape(1024, 256),
            )
            if first:
                pacc[j, near_rows] = t
            else:
                pacc[j, near_rows] += t

    recv(group(x, 1 - c), ("S", 0), sibling)
    project_group(x, True)
    recv(group(xn, 1 - c), ("S", -1), sibling)
    project_group(xn, False)
    recv(unit(x2, zh), ("W", 2, 0), xm)
    recv(unit(x2, zn), ("W", 2, -1), xm)
    recv(unit(x2, zq), ("W", 2, 1), xp)
    recv(unit(x2, z2), ("W", 2, 2), xp)
    pass_on(group(x2, c), ("S", 2), sibling)
    recv(group(xq, 1 - c), ("S", 1), sibling)
    project_group(xq, False)
    recv(group(x2, 1 - c), ("S", 2), sibling)
    project_group(x2, False)

    def place_rows(j, dy, dz, p):
        r = rows(ring(y, dy), zl if dz == 0 else 1 - zl)
        rotated = j < 2
        cc = jnp.where(rotated, cosv[r], 1.0)
        ss = jnp.where(rotated, sinv[r], 0.0)
        for h in range(2):
            ph = p[:, h * HS:(h + 1) * HS]
            qkv[j, h, r] = (ph * cc + pltpu.roll(ph, 64, 1) * ss).astype(BF16)

    @pl.loop(0, 3)
    def _(j):
        for dy in (1, -1, 0):
            for dz in range(2):
                place_rows(j, dy, dz, pacc[j, slot(dy, dz)])

    recv(xpiece(2, 0, cols(0)), ("Xr", 0, 0), ym)
    recv(xpiece(2, 0, cols(1)), ("Xr", 0, 1), yp)
    for k in (0, 1):
        recv(xpiece(2, 1, quarter(k)), ("Xr", 1, k), ym)
    for k in (2, 3):
        recv(xpiece(2, 1, quarter(k)), ("Xr", 1, k), yp)

    @pl.loop(0, 3)
    def _(j):
        p = dot_nn(xv[pl.ds(0, 160)], wv[j].reshape(D, 256))
        for dz in range(2):
            place_rows(j, 2, dz, p[dz * 80:(dz + 1) * 80])

    scale = HS ** -0.5
    lower = lax.broadcasted_iota(jnp.int32, (128, 128), 0) >= lax.broadcasted_iota(
        jnp.int32, (128, 128), 1
    )

    def rotate_back(v, r):
        return (v * cosv[r] - pltpu.roll(v, 64, 1) * sinv[r]).astype(BF16)

    heads = range(2)
    for i in reversed(range(5)):
        n = (i + 1) * 128
        r, head = pl.ds(i * 128, 128), pl.ds(0, n)
        q = [qkv[0, h, r] for h in heads]
        k = [qkv[1, h, head] for h in heads]
        v = [qkv[2, h, head] for h in heads]
        up = [upv[r, pl.ds(h * HS, HS)] for h in heads]
        s = [dot_nt(q[h], k[h]) for h in heads]
        gp = [dot_nt(up[h], v[h]) for h in heads]
        low, gs = [], []
        for h in heads:
            diagonal = jnp.where(lower, s[h][:, i * 128:], -1e30)
            if i:
                diagonal = jnp.concatenate([s[h][:, : i * 128], diagonal], 1)
            top_score = jnp.max(diagonal, 1, keepdims=True)
            e = jnp.exp2((diagonal - top_score) * (scale * np.log2(np.e)))
            prob = e * (1.0 / jnp.sum(e, 1, keepdims=True))
            low.append(prob.astype(BF16))
            dots = jnp.sum(low[h].astype(F32) * gp[h], 1, keepdims=True)
            gs.append((prob * (gp[h] - dots)).astype(BF16))
        for h in heads:
            gv[r, pl.ds(h * HS, HS)] = rotate_back(dot_nn(gs[h], k[h]) * scale, r)
            dk, dv = dot_tn(gs[h], q[h]), dot_tn(low[h], up[h])
            if i == 4:
                accv[h], accv[2 + h] = dk, dv
            else:
                accv[h, head] += dk
                accv[2 + h, head] += dv
    full = pl.ds(0, SEQ)
    for h in heads:
        gv[:, pl.ds(256 + h * HS, HS)] = rotate_back(accv[h] * scale, full)
        gv[:, pl.ds(512 + h * HS, HS)] = accv[2 + h].astype(BF16)
    for dy in POSITION:
        for dz in range(2):
            gr[slot(dy, dz)] = gv[rows(ring(y, dy), zl if dz == 0 else 1 - zl)]

    def x_term(first, count):
        r = pl.ds(first, count)

        @pl.loop(0, 4)
        def _(i):
            total = None
            for j in range(3):
                w = wv[j, pl.ds(i * 4, 4)].reshape(1024, 256)
                t = dot_nt(gr[r, pl.ds(j * 256, 256)], w)
                total = t if total is None else total + t
            dxp[r, pl.ds(pl.multiple_of(i * 1024, 1024), 1024)] = total.astype(BF16)

    def w_term(xx):
        @pl.loop(0, 4)
        def _(i):
            b = xx * 4 + i
            t = dot_tn(xv[:, pl.ds(pl.multiple_of(b * 256, 256), 256)], gr[...])
            for cc in range(2):
                for j in range(3):
                    dwp[b, cc, j] = t[cc * 128:(cc + 1) * 128, j * 256:(j + 1) * 256].astype(BF16)

    def add_into(dst, src):
        dst[...] = (dst[...].astype(F32) + src[...].astype(F32)).astype(BF16)

    def add_two(dst, one, two):
        dst[...] = (
            dst[...].astype(F32) + one[...].astype(F32) + two[...].astype(F32)
        ).astype(BF16)

    def xpart(dy, dz, part):
        return dxp.at[slot(dy, dz), part]

    def wunit(xx, zz):
        return dwp.at[xx * 4 + zz, c]

    def send_sib(xx, dx):
        send(dwp.at[pl.ds(xx * 4, 4), 1 - c], sib_v.at[pl.ds(xx * 4, 4)], ("DS", dx), sibling)

    def recv_sib(xx, dx):
        recv(sib_v.at[pl.ds(xx * 4, 4)], ("DS", dx), sibling)

        @pl.loop(0, 4)
        def _(i):
            add_into(dwp.at[xx * 4 + i, c], sib_v.at[xx * 4 + i])

    def far_x(dz):
        send(xpart(2, dz, cols(0)), rel_v.at[0, dz], ("R", 0, dz), yp)
        send(xpart(2, dz, cols(1)), rel_v.at[1, dz], ("R", 1, dz), ym)

    def near_x(s, dz, h):
        dy, device = ((1, yp), (-1, ym))[s]
        send(xpart(dy, dz, cols(h)), fin_v.at[s, dz, h], ("F", s, dz, h), device)

    def relay_x(dz):
        recv(rel_v.at[0, dz], ("R", 0, dz), ym)
        add_into(xpart(1, dz, cols(0)), rel_v.at[0, dz])
        near_x(0, dz, 0)
        recv(rel_v.at[1, dz], ("R", 1, dz), yp)
        add_into(xpart(-1, dz, cols(1)), rel_v.at[1, dz])
        near_x(1, dz, 1)

    def recv_near(s, dz, h):
        recv(fin_v.at[s, dz, h], ("F", s, dz, h), (ym, yp)[s])

    up_units, down_units = (2, -1), (1, 0)
    zs = {0: zh, 1: zq, 2: z2, -1: zn}

    def far_w(dz):
        if dz in up_units:
            send(wunit(x2, zs[dz]), xrel_v.at[zs[dz]], ("XR", dz), xp)
        else:
            send(wunit(x2, zs[dz]), xrel_v.at[zs[dz]], ("XR", dz), xm)

    def relay_w(dz):
        if dz in up_units:
            recv(xrel_v.at[zs[dz]], ("XR", dz), xm)
            add_into(wunit(xq, zs[dz]), xrel_v.at[zs[dz]])
        else:
            recv(xrel_v.at[zs[dz]], ("XR", dz), xp)
            add_into(wunit(xn, zs[dz]), xrel_v.at[zs[dz]])

    def near_w(dz):
        relay_w(dz)
        send(wunit(xq, zs[dz]), xfin_v.at[0, zs[dz]], ("XF", 0, dz), xp)
        send(wunit(xn, zs[dz]), xfin_v.at[1, zs[dz]], ("XF", 1, dz), xm)

    def sum_w(dz):
        recv(xfin_v.at[0, zs[dz]], ("XF", 0, dz), xm)
        recv(xfin_v.at[1, zs[dz]], ("XF", 1, dz), xp)
        add_two(wunit(x, zs[dz]), xfin_v.at[0, zs[dz]], xfin_v.at[1, zs[dz]])

    def wz_half(zz, part):
        return dwp.at[x * 4 + zz, c, :, part]

    def mate_x(h):
        add_two(xpart(0, 1, cols(h)), fin_v.at[0, 1, h], fin_v.at[1, 1, h])
        send(xpart(0, 1, cols(h)), zl_v.at[h], ("Z", h), mate)

    x_term(0, 160)
    far_x(1)
    w_term(x2)
    send_sib(x2, 2)
    x_term(160, 480)
    near_x(0, 1, 1)
    near_x(1, 1, 0)
    recv_sib(x2, 2)
    far_w(2)
    far_w(1)
    w_term(xq)
    send_sib(xq, 1)
    w_term(xn)
    send_sib(xn, -1)
    relay_x(1)
    recv_sib(xq, 1)
    recv_sib(xn, -1)
    near_w(2)
    w_term(x)
    send_sib(x, 0)
    near_w(1)
    far_w(-1)
    far_w(0)
    recv_near(0, 1, 1)
    recv_near(1, 1, 0)
    far_x(0)
    recv_sib(x, 0)
    sum_w(2)
    send(wz_half(z2, top), zrel_v.at[0], ("ZR", 0), zp)
    send(wz_half(z2, bottom), zrel_v.at[1], ("ZR", 1), zm)
    recv_near(0, 1, 0)
    mate_x(0)
    recv_near(1, 1, 1)
    mate_x(1)
    near_x(0, 0, 1)
    near_x(1, 0, 0)
    near_w(-1)
    sum_w(1)
    send(wz_half(zq, bottom), zfin_v.at[0, :, bottom], ("ZF", 0, 1), zp)
    near_w(0)
    sum_w(-1)
    send(wz_half(zn, top), zfin_v.at[1, :, top], ("ZF", 1, 0), zm)
    recv(zrel_v.at[0], ("ZR", 0), zm)
    add_into(wz_half(zq, top), zrel_v.at[0])
    send(wz_half(zq, top), zfin_v.at[0, :, top], ("ZF", 0, 0), zp)
    recv(zrel_v.at[1], ("ZR", 1), zp)
    add_into(wz_half(zn, bottom), zrel_v.at[1])
    send(wz_half(zn, bottom), zfin_v.at[1, :, bottom], ("ZF", 1, 1), zm)
    relay_x(0)
    sum_w(0)

    recv(zfin_v.at[0, :, bottom], ("ZF", 0, 1), zm)
    recv(zfin_v.at[0, :, top], ("ZF", 0, 0), zm)
    recv(zfin_v.at[1, :, top], ("ZF", 1, 0), zp)
    recv(zfin_v.at[1, :, bottom], ("ZF", 1, 1), zp)
    dw_out[...] = (
        wunit(x, zh)[...].astype(F32) + zfin_v[0].astype(F32) + zfin_v[1].astype(F32)
    )

    for h in range(2):
        recv(zl_v.at[h], ("Z", h), mate)
        recv_near(0, 0, h)
        recv_near(1, 0, h)
        dx_out[:, h * HALF:(h + 1) * HALF] = (
            xpart(0, 0, cols(h))[...].astype(F32)
            + fin_v[0, 0, h].astype(F32)
            + fin_v[1, 0, h].astype(F32)
            + zl_v[h].astype(F32)
        ).astype(BF16)

    for copy in sends:
        copy.wait_send()
    assert len(sends) <= N_SEND and len(keys) <= N_RECV


def shards(inputs, projections, upstream_grad):
    cosine, sine = rotary_tables()
    any_spec = pl.BlockSpec(memory_space=pl.ANY)
    vmem = pl.BlockSpec(memory_space=pltpu.VMEM)
    return pl.pallas_call(
        kernel,
        out_shape=(
            jax.ShapeDtypeStruct((80, D), BF16),
            jax.ShapeDtypeStruct((3, 128, 256), F32),
        ),
        in_specs=[any_spec] * 5,
        out_specs=(vmem, vmem),
        scratch_shapes=[
            pltpu.VMEM((SEQ, D), BF16),
            pltpu.VMEM((3, 16, 2, 128, 256), BF16),
            pltpu.VMEM((SEQ, 256), BF16),
            pltpu.VMEM((SEQ, HS), F32),
            pltpu.VMEM((SEQ, HS), F32),
            pltpu.VMEM((3, SEQ, 256), F32),
            pltpu.VMEM((3, 2, SEQ, HS), BF16),
            pltpu.VMEM((SEQ, 768), BF16),
            pltpu.VMEM((SEQ, 768), BF16),
            pltpu.VMEM((4, SEQ, HS), F32),
            pltpu.VMEM((SEQ, D), BF16),
            pltpu.VMEM((16, 2, 3, 128, 256), BF16),
            pltpu.VMEM((2, 2, 80, HALF), BF16),
            pltpu.VMEM((2, 2, 2, 80, HALF), BF16),
            pltpu.VMEM((2, 80, HALF), BF16),
            pltpu.VMEM((16, 3, 128, 256), BF16),
            pltpu.VMEM((4, 3, 128, 256), BF16),
            pltpu.VMEM((2, 4, 3, 128, 256), BF16),
            pltpu.VMEM((2, 3, 64, 256), BF16),
            pltpu.VMEM((2, 3, 128, 256), BF16),
            pltpu.SemaphoreType.DMA((N_SEND,)),
            pltpu.SemaphoreType.DMA((N_RECV,)),
            pltpu.SemaphoreType.DMA((5,)),
        ],
        compiler_params=pltpu.CompilerParams(
            collective_id=0, has_side_effects=True, vmem_limit_bytes=60 * 2**20
        ),
        name="mixer_backward",
    )(inputs, projections, upstream_grad, jnp.asarray(cosine), jnp.asarray(sine))


def solution(mesh):
    return jax.shard_map(
        shards,
        mesh=mesh,
        in_specs=(P(("dp", "tensor"), None), P(None, "dp", "tensor"), P("dp", "tensor")),
        out_specs=(P(("dp", "tensor"), None), P(None, "dp", "tensor")),
        check_vma=False,
    )
```

```python
import functools

import jax
import jax.numpy as jnp
import numpy as np
from jax import lax
from jax.experimental import pallas as pl
from jax.experimental.pallas import tpu as pltpu
from jax.sharding import PartitionSpec as P

HS = 128
SEQ = 640
D = 4096
MESH = pl.DeviceIdType.MESH
F32 = jnp.float32
BF16 = jnp.bfloat16
HALF = D // 2
MIDDLE = pl.ds(1536, 1024)
POSITION = {2: 0, 1: 1, -1: 2, 0: 3}


def rotary_tables():
    half = HS // 2
    frequency = 10000.0 ** (-np.arange(half, dtype=np.float64) / half)
    angles = np.arange(SEQ, dtype=np.float64)[:, None] * frequency[None, :]
    cosine, sine = np.cos(angles), np.sin(angles)
    return (
        np.concatenate([cosine, cosine], -1).astype(np.float32),
        np.concatenate([-sine, sine], -1).astype(np.float32),
    )


def dot_nn(a, b):
    return lax.dot_general(a, b, (((1,), (0,)), ((), ())), preferred_element_type=F32)


def dot_nt(a, b):
    return lax.dot_general(a, b, (((1,), (1,)), ((), ())), preferred_element_type=F32)


def dot_tn(a, b):
    return lax.dot_general(a, b, (((0,), (0,)), ((), ())), preferred_element_type=F32)


N_SEND = 96
N_RECV = 96


def kernel(
    x_in, w_in, up_in, cos_in, sin_in, dx_out, dw_out,
    xv, wv, upv, cosv, sinv, pacc, qkv, gv, gr, accv, dxp, dwp,
    rel_v, fin_v, zl_v, zb_v, sib_v, xrel_v, xfin_v, zrel_v, zfin_v,
    send_sem, recv_sem, local_sem,
):
    dp = lax.axis_index("dp")
    tensor = lax.axis_index("tensor")
    x, zh, c = dp // 8, (dp // 2) % 4, dp % 2
    y, zl = tensor // 2, tensor % 2

    def place(xx, zz, cc, yy, ll):
        return {"dp": xx * 8 + zz * 2 + cc, "tensor": yy * 2 + ll}

    def ring(v, step):
        return lax.rem(v + (step + 4), 4)

    yp, ym = place(x, zh, c, ring(y, 1), zl), place(x, zh, c, ring(y, -1), zl)
    xp, xm = place(ring(x, 1), zh, c, y, zl), place(ring(x, -1), zh, c, y, zl)
    zp, zm = place(x, ring(zh, 1), c, y, zl), place(x, ring(zh, -1), c, y, zl)
    mate = place(x, zh, c, y, 1 - zl)
    sibling = place(x, zh, 1 - c, y, zl)
    everyone = (yp, ym, xp, xm, zp, zm, mate, sibling)

    keys = {}
    sends = []

    def key_index(key):
        return keys.setdefault(key, len(keys))

    def send(src, dst, key, device):
        copy = pltpu.make_async_remote_copy(
            src_ref=src, dst_ref=dst, send_sem=send_sem.at[len(sends)],
            recv_sem=recv_sem.at[key_index(key)], device_id=device, device_id_type=MESH,
        )
        copy.start()
        sends.append(copy)

    def recv(dst, key, device):
        pltpu.make_async_remote_copy(
            src_ref=dst, dst_ref=dst, send_sem=send_sem.at[0],
            recv_sem=recv_sem.at[key_index(key)], device_id=device, device_id_type=MESH,
        ).wait_recv()

    def rows(yy, ll):
        return pl.ds(pl.multiple_of(yy * 160 + ll * 80, 16), 80)

    def cols(h):
        return pl.ds(h * HALF, HALF)

    def slot(dy, dz):
        return pl.ds(160 * POSITION[dy] + 80 * dz, 80)

    own_x = xv.at[slot(0, 0)]

    def unit(xx, zz):
        return wv.at[:, xx * 4 + zz, c]

    locals_ = [
        pltpu.make_async_copy(x_in, own_x, local_sem.at[0]),
        pltpu.make_async_copy(w_in, unit(x, zh), local_sem.at[1]),
        pltpu.make_async_copy(up_in, upv, local_sem.at[2]),
        pltpu.make_async_copy(cos_in, cosv, local_sem.at[3]),
        pltpu.make_async_copy(sin_in, sinv, local_sem.at[4]),
    ]
    for copy in locals_:
        copy.start()

    barrier = pltpu.get_barrier_semaphore()
    for device in everyone:
        pl.semaphore_signal(barrier, inc=1, device_id=device, device_id_type=MESH)
    pl.semaphore_wait(barrier, len(everyone))

    top, bottom = pl.ds(0, 64), pl.ds(64, 64)

    def unit_half(xx, zz, part):
        return wv.at[:, xx * 4 + zz, c, part]

    def group(xx, cc):
        return wv.at[:, pl.ds(xx * 4, 4), cc]

    xn, xq, x2 = ring(x, -1), ring(x, 1), ring(x, 2)
    zn, zq, z2 = ring(zh, -1), ring(zh, 1), ring(zh, 2)

    def quarter(k):
        return pl.ds((0, 768, 2560, 3328)[k], 768)

    def xpiece(dy, dz, part):
        return xv.at[slot(dy, dz), part]

    def to_mate(k):
        send(x_in.at[:, quarter(k)], xpiece(0, 1, quarter(k)), ("Xp", k), mate)

    to_mate(0)
    to_mate(2)
    send(w_in, unit(x, zh), ("W", 0, -1), zp)
    send(w_in, unit(x, zh), ("W", 0, 1), zm)
    for h in range(2):
        send(x_in.at[:, cols(h)], xpiece(-1, 0, cols(h)), ("Xo", -1, h), yp)
        send(x_in.at[:, cols(1 - h)], xpiece(1, 0, cols(1 - h)), ("Xo", 1, 1 - h), ym)
    send(w_in, unit(x, zh), ("W", -1, 0), xp)
    send(w_in, unit(x, zh), ("W", 1, 0), xm)
    for copy in locals_:
        copy.wait()

    def pass_on(piece, key, device):
        send(piece, piece, key, device)

    def mate_piece(k):
        piece = xpiece(0, 1, quarter(k))
        recv(piece, ("Xp", k), mate)
        send(piece, xpiece(-1, 1, quarter(k)), ("Xq", -1, k), yp)
        send(piece, xpiece(1, 1, quarter(k)), ("Xq", 1, k), ym)

    def far_piece(k):
        dy, source, device = (-1, ym, yp) if k < 2 else (1, yp, ym)
        piece = xpiece(dy, 1, quarter(k))
        recv(piece, ("Xq", dy, k), source)
        send(piece, xpiece(2, 1, quarter(k)), ("Xr", 1, k), device)

    recv(unit(xn, zh), ("W", -1, 0), xm)
    pass_on(unit(xn, zh), ("W", 2, 0), xp)
    recv(unit(xq, zh), ("W", 1, 0), xp)

    mate_piece(0)
    mate_piece(2)
    to_mate(1)
    to_mate(3)
    recv(unit(x, zn), ("W", 0, -1), zm)
    pass_on(unit_half(x, zn, top), "WrA", zp)
    pass_on(unit(x, zn), ("W", -1, -1), xp)
    pass_on(unit(x, zn), ("W", 1, -1), xm)
    recv(unit(x, zq), ("W", 0, 1), zp)
    pass_on(unit_half(x, zq, bottom), "WrB", zm)
    pass_on(unit(x, zq), ("W", -1, 1), xp)
    pass_on(unit(x, zq), ("W", 1, 1), xm)

    recv(xpiece(-1, 0, cols(0)), ("Xo", -1, 0), ym)
    send(xpiece(-1, 0, cols(0)), xpiece(2, 0, cols(0)), ("Xr", 0, 0), yp)
    recv(xpiece(1, 0, cols(1)), ("Xo", 1, 1), yp)
    send(xpiece(1, 0, cols(1)), xpiece(2, 0, cols(1)), ("Xr", 0, 1), ym)

    def middle_piece(dy):
        send(xpiece(dy, 0, MIDDLE), xpiece(dy, 1, MIDDLE), ("Xb", dy), mate)


    recv(unit_half(x, z2, top), "WrA", zm)
    recv(unit_half(x, z2, bottom), "WrB", zp)
    pass_on(unit(x, z2), ("W", -1, 2), xp)
    pass_on(unit(x, z2), ("W", 1, 2), xm)
    pass_on(group(x, c), ("S", 0), sibling)
    mate_piece(1)
    mate_piece(3)
    middle_piece(0)
    recv(xpiece(-1, 0, cols(1)), ("Xo", -1, 1), ym)
    middle_piece(-1)
    recv(xpiece(1, 0, cols(0)), ("Xo", 1, 0), yp)
    middle_piece(1)

    recv(unit(xn, zn), ("W", -1, -1), xm)
    pass_on(unit(xn, zn), ("W", 2, -1), xp)
    recv(unit(xq, zq), ("W", 1, 1), xp)
    pass_on(unit(xq, zq), ("W", 2, 1), xm)
    far_piece(0)
    far_piece(2)
    recv(unit(xq, zn), ("W", 1, -1), xp)
    recv(unit(xn, zq), ("W", -1, 1), xm)
    recv(unit(xq, z2), ("W", 1, 2), xp)
    pass_on(unit(xq, z2), ("W", 2, 2), xm)
    recv(unit(xn, z2), ("W", -1, 2), xm)
    pass_on(group(xn, c), ("S", -1), sibling)
    pass_on(group(xq, c), ("S", 1), sibling)
    far_piece(1)
    far_piece(3)

    recv(xpiece(2, 0, cols(0)), ("Xr", 0, 0), ym)
    recv(xpiece(2, 0, cols(1)), ("Xr", 0, 1), yp)
    middle_piece(2)
    for dy in (0, -1, 1):
        recv(xpiece(dy, 1, MIDDLE), ("Xb", dy), mate)
    for k in (2, 3):
        recv(xpiece(-1, 1, quarter(k)), ("Xq", -1, k), ym)
    for k in (0, 1):
        recv(xpiece(1, 1, quarter(k)), ("Xq", 1, k), yp)
    near_rows = pl.ds(160, 480)

    def project_group(xx, first):
        @pl.loop(0, 3)
        def _(j):
            t = dot_nn(
                xv[near_rows, pl.ds(pl.multiple_of(xx * 1024, 1024), 1024)],
                wv[j, pl.ds(xx * 4, 4)].reshape(1024, 256),
            )
            if first:
                pacc[j, near_rows] = t
            else:
                pacc[j, near_rows] += t

    recv(group(x, 1 - c), ("S", 0), sibling)
    project_group(x, True)
    recv(group(xn, 1 - c), ("S", -1), sibling)
    project_group(xn, False)
    recv(unit(x2, zh), ("W", 2, 0), xm)
    recv(unit(x2, zn), ("W", 2, -1), xm)
    recv(unit(x2, zq), ("W", 2, 1), xp)
    recv(unit(x2, z2), ("W", 2, 2), xp)
    pass_on(group(x2, c), ("S", 2), sibling)
    recv(group(xq, 1 - c), ("S", 1), sibling)
    project_group(xq, False)
    recv(group(x2, 1 - c), ("S", 2), sibling)
    project_group(x2, False)

    def place_rows(j, dy, dz, p):
        r = rows(ring(y, dy), zl if dz == 0 else 1 - zl)
        rotated = j < 2
        cc = jnp.where(rotated, cosv[r], 1.0)
        ss = jnp.where(rotated, sinv[r], 0.0)
        for h in range(2):
            ph = p[:, h * HS:(h + 1) * HS]
            qkv[j, h, r] = (ph * cc + pltpu.roll(ph, 64, 1) * ss).astype(BF16)

    @pl.loop(0, 3)
    def _(j):
        for dy in (1, -1, 0):
            for dz in range(2):
                place_rows(j, dy, dz, pacc[j, slot(dy, dz)])

    recv(xpiece(2, 1, MIDDLE), ("Xb", 2), mate)
    for k in (0, 1):
        recv(xpiece(2, 1, quarter(k)), ("Xr", 1, k), ym)
    for k in (2, 3):
        recv(xpiece(2, 1, quarter(k)), ("Xr", 1, k), yp)

    @pl.loop(0, 3)
    def _(j):
        p = dot_nn(xv[pl.ds(0, 160)], wv[j].reshape(D, 256))
        for dz in range(2):
            place_rows(j, 2, dz, p[dz * 80:(dz + 1) * 80])

    scale = HS ** -0.5
    lower = lax.broadcasted_iota(jnp.int32, (128, 128), 0) >= lax.broadcasted_iota(
        jnp.int32, (128, 128), 1
    )

    def rotate_back(v, r):
        return (v * cosv[r] - pltpu.roll(v, 64, 1) * sinv[r]).astype(BF16)

    heads = range(2)
    for i in reversed(range(5)):
        n = (i + 1) * 128
        r, head = pl.ds(i * 128, 128), pl.ds(0, n)
        q = [qkv[0, h, r] for h in heads]
        k = [qkv[1, h, head] for h in heads]
        v = [qkv[2, h, head] for h in heads]
        up = [upv[r, pl.ds(h * HS, HS)] for h in heads]
        s = [dot_nt(q[h], k[h]) for h in heads]
        gp = [dot_nt(up[h], v[h]) for h in heads]
        low, gs = [], []
        for h in heads:
            diagonal = jnp.where(lower, s[h][:, i * 128:], -1e30)
            if i:
                diagonal = jnp.concatenate([s[h][:, : i * 128], diagonal], 1)
            top_score = jnp.max(diagonal, 1, keepdims=True)
            e = jnp.exp2((diagonal - top_score) * (scale * np.log2(np.e)))
            prob = e * (1.0 / jnp.sum(e, 1, keepdims=True))
            low.append(prob.astype(BF16))
            dots = jnp.sum(low[h].astype(F32) * gp[h], 1, keepdims=True)
            gs.append((prob * (gp[h] - dots)).astype(BF16))
        for h in heads:
            gv[r, pl.ds(h * HS, HS)] = rotate_back(dot_nn(gs[h], k[h]) * scale, r)
            dk, dv = dot_tn(gs[h], q[h]), dot_tn(low[h], up[h])
            if i == 4:
                accv[h], accv[2 + h] = dk, dv
            else:
                accv[h, head] += dk
                accv[2 + h, head] += dv
    full = pl.ds(0, SEQ)
    for h in heads:
        gv[:, pl.ds(256 + h * HS, HS)] = rotate_back(accv[h] * scale, full)
        gv[:, pl.ds(512 + h * HS, HS)] = accv[2 + h].astype(BF16)
    for dy in POSITION:
        for dz in range(2):
            gr[slot(dy, dz)] = gv[rows(ring(y, dy), zl if dz == 0 else 1 - zl)]

    def x_term(first, count, part):
        r, depth = pl.ds(first, count), part.size
        total = None
        for j in range(3):
            w = wv[j, pl.ds(part.start // 256, depth // 256)].reshape(depth, 256)
            t = dot_nt(gr[r, pl.ds(j * 256, 256)], w)
            total = t if total is None else total + t
        dxp[r, part] = total.astype(BF16)

    def w_term(xx):
        @pl.loop(0, 4)
        def _(i):
            b = xx * 4 + i
            t = dot_tn(xv[:, pl.ds(pl.multiple_of(b * 256, 256), 256)], gr[...])
            for cc in range(2):
                for j in range(3):
                    dwp[b, cc, j] = t[cc * 128:(cc + 1) * 128, j * 256:(j + 1) * 256].astype(BF16)

    def add_into(dst, src):
        dst[...] = (dst[...].astype(F32) + src[...].astype(F32)).astype(BF16)

    def add_two(dst, one, two):
        dst[...] = (
            dst[...].astype(F32) + one[...].astype(F32) + two[...].astype(F32)
        ).astype(BF16)

    def xpart(dy, dz, part):
        return dxp.at[slot(dy, dz), part]

    def wunit(xx, zz):
        return dwp.at[xx * 4 + zz, c]

    def send_sib(xx, dx):
        send(dwp.at[pl.ds(xx * 4, 4), 1 - c], sib_v.at[pl.ds(xx * 4, 4)], ("DS", dx), sibling)

    def recv_sib(xx, dx):
        recv(sib_v.at[pl.ds(xx * 4, 4)], ("DS", dx), sibling)

        @pl.loop(0, 4)
        def _(i):
            add_into(dwp.at[xx * 4 + i, c], sib_v.at[xx * 4 + i])

    def side(h, dz):
        if dz == 0:
            return cols(h)
        return pl.ds((0, 2560)[h], 1536)

    def kept(dz):
        return pl.ds(0, HALF if dz == 0 else 1536)

    def far_x(h, p):
        send(
            xpart(2, 1, quarter(2 * h + p)), rel_v.at[h, 1, :, pl.ds(768 * p, 768)],
            ("R", h, 1, p), (yp, ym)[h],
        )

    def near_x(s, dz, h):
        dy, device = ((1, yp), (-1, ym))[s]
        send(xpart(dy, dz, side(h, dz)), fin_v.at[s, dz, h, :, kept(dz)], ("F", s, dz, h), device)

    def relay_x(dz):
        for h, dy, source in ((0, 1, ym), (1, -1, yp)):
            if dz == 0:
                recv(rel_v.at[h, 0], ("R", h, 0), source)
            else:
                for p in range(2):
                    recv(rel_v.at[h, 1, :, pl.ds(768 * p, 768)], ("R", h, 1, p), source)
            add_into(xpart(dy, dz, side(h, dz)), rel_v.at[h, dz, :, kept(dz)])
            near_x(h, dz, h)

    def middle_x(dy):
        send(xpart(dy, 1, MIDDLE), zb_v.at[POSITION[dy]], ("ZB", dy), mate)

    def add_middle(dy):
        recv(zb_v.at[POSITION[dy]], ("ZB", dy), mate)
        add_into(xpart(dy, 0, MIDDLE), zb_v.at[POSITION[dy]])

    def recv_near(s, dz, h):
        recv(fin_v.at[s, dz, h, :, kept(dz)], ("F", s, dz, h), (ym, yp)[s])

    up_units, down_units = (2, -1), (1, 0)
    zs = {0: zh, 1: zq, 2: z2, -1: zn}

    def far_w(dz):
        if dz in up_units:
            send(wunit(x2, zs[dz]), xrel_v.at[zs[dz]], ("XR", dz), xp)
        else:
            send(wunit(x2, zs[dz]), xrel_v.at[zs[dz]], ("XR", dz), xm)

    def relay_w(dz):
        if dz in up_units:
            recv(xrel_v.at[zs[dz]], ("XR", dz), xm)
            add_into(wunit(xq, zs[dz]), xrel_v.at[zs[dz]])
        else:
            recv(xrel_v.at[zs[dz]], ("XR", dz), xp)
            add_into(wunit(xn, zs[dz]), xrel_v.at[zs[dz]])

    def near_w(dz):
        relay_w(dz)
        send(wunit(xq, zs[dz]), xfin_v.at[0, zs[dz]], ("XF", 0, dz), xp)
        send(wunit(xn, zs[dz]), xfin_v.at[1, zs[dz]], ("XF", 1, dz), xm)

    def sum_w(dz):
        recv(xfin_v.at[0, zs[dz]], ("XF", 0, dz), xm)
        recv(xfin_v.at[1, zs[dz]], ("XF", 1, dz), xp)
        add_two(wunit(x, zs[dz]), xfin_v.at[0, zs[dz]], xfin_v.at[1, zs[dz]])

    def wz_half(zz, part):
        return dwp.at[x * 4 + zz, c, :, part]

    def mate_x(h):
        part = xpart(0, 1, side(h, 1))
        add_two(part, fin_v.at[0, 1, h, :, kept(1)], fin_v.at[1, 1, h, :, kept(1)])
        send(part, zl_v.at[h], ("Z", h), mate)

    for p in range(2):
        for h in range(2):
            x_term(0, 160, quarter(2 * h + p))
            far_x(h, p)
    x_term(0, SEQ, MIDDLE)
    for dy in POSITION:
        middle_x(dy)
    w_term(x2)
    send_sib(x2, 2)
    for k in range(4):
        x_term(160, 480, quarter(k))
    near_x(0, 1, 1)
    near_x(1, 1, 0)
    recv_sib(x2, 2)
    far_w(2)
    far_w(1)
    w_term(xq)
    send_sib(xq, 1)
    w_term(xn)
    send_sib(xn, -1)
    relay_x(1)
    recv_sib(xq, 1)
    recv_sib(xn, -1)
    near_w(2)
    w_term(x)
    send_sib(x, 0)
    near_w(1)
    far_w(-1)
    far_w(0)
    recv_near(0, 1, 1)
    recv_near(1, 1, 0)
    add_middle(2)
    send(xpart(2, 0, cols(0)), rel_v.at[0, 0], ("R", 0, 0), yp)
    send(xpart(2, 0, cols(1)), rel_v.at[1, 0], ("R", 1, 0), ym)
    recv_sib(x, 0)
    sum_w(2)
    send(wz_half(z2, top), zrel_v.at[0], ("ZR", 0), zp)
    send(wz_half(z2, bottom), zrel_v.at[1], ("ZR", 1), zm)
    recv_near(0, 1, 0)
    mate_x(0)
    recv_near(1, 1, 1)
    mate_x(1)
    add_middle(1)
    add_middle(-1)
    near_x(0, 0, 1)
    near_x(1, 0, 0)
    add_middle(0)
    near_w(-1)
    sum_w(1)
    send(wz_half(zq, bottom), zfin_v.at[0, :, bottom], ("ZF", 0, 1), zp)
    near_w(0)
    sum_w(-1)
    send(wz_half(zn, top), zfin_v.at[1, :, top], ("ZF", 1, 0), zm)
    recv(zrel_v.at[0], ("ZR", 0), zm)
    add_into(wz_half(zq, top), zrel_v.at[0])
    send(wz_half(zq, top), zfin_v.at[0, :, top], ("ZF", 0, 0), zp)
    recv(zrel_v.at[1], ("ZR", 1), zp)
    add_into(wz_half(zn, bottom), zrel_v.at[1])
    send(wz_half(zn, bottom), zfin_v.at[1, :, bottom], ("ZF", 1, 1), zm)
    relay_x(0)
    sum_w(0)

    recv(zfin_v.at[0, :, bottom], ("ZF", 0, 1), zm)
    recv(zfin_v.at[0, :, top], ("ZF", 0, 0), zm)
    recv(zfin_v.at[1, :, top], ("ZF", 1, 0), zp)
    recv(zfin_v.at[1, :, bottom], ("ZF", 1, 1), zp)
    dw_out[...] = (
        wunit(x, zh)[...].astype(F32) + zfin_v[0].astype(F32) + zfin_v[1].astype(F32)
    )

    for h in range(2):
        recv(zl_v.at[h], ("Z", h), mate)
        recv_near(0, 0, h)
        recv_near(1, 0, h)
        total = (
            xpart(0, 0, cols(h))[...].astype(F32)
            + fin_v[0, 0, h].astype(F32)
            + fin_v[1, 0, h].astype(F32)
        )
        if h == 0:
            dx_out[:, :1536] = (total[:, :1536] + zl_v[0].astype(F32)).astype(BF16)
            dx_out[:, 1536:HALF] = total[:, 1536:].astype(BF16)
        else:
            dx_out[:, HALF:2560] = total[:, :512].astype(BF16)
            dx_out[:, 2560:] = (total[:, 512:] + zl_v[1].astype(F32)).astype(BF16)

    for copy in sends:
        copy.wait_send()
    assert len(sends) <= N_SEND and len(keys) <= N_RECV


def shards(inputs, projections, upstream_grad):
    cosine, sine = rotary_tables()
    any_spec = pl.BlockSpec(memory_space=pl.ANY)
    vmem = pl.BlockSpec(memory_space=pltpu.VMEM)
    return pl.pallas_call(
        kernel,
        out_shape=(
            jax.ShapeDtypeStruct((80, D), BF16),
            jax.ShapeDtypeStruct((3, 128, 256), F32),
        ),
        in_specs=[any_spec] * 5,
        out_specs=(vmem, vmem),
        scratch_shapes=[
            pltpu.VMEM((SEQ, D), BF16),
            pltpu.VMEM((3, 16, 2, 128, 256), BF16),
            pltpu.VMEM((SEQ, 256), BF16),
            pltpu.VMEM((SEQ, HS), F32),
            pltpu.VMEM((SEQ, HS), F32),
            pltpu.VMEM((3, SEQ, 256), F32),
            pltpu.VMEM((3, 2, SEQ, HS), BF16),
            pltpu.VMEM((SEQ, 768), BF16),
            pltpu.VMEM((SEQ, 768), BF16),
            pltpu.VMEM((4, SEQ, HS), F32),
            pltpu.VMEM((SEQ, D), BF16),
            pltpu.VMEM((16, 2, 3, 128, 256), BF16),
            pltpu.VMEM((2, 2, 80, HALF), BF16),
            pltpu.VMEM((2, 2, 2, 80, HALF), BF16),
            pltpu.VMEM((2, 80, 1536), BF16),
            pltpu.VMEM((4, 80, 1024), BF16),
            pltpu.VMEM((16, 3, 128, 256), BF16),
            pltpu.VMEM((4, 3, 128, 256), BF16),
            pltpu.VMEM((2, 4, 3, 128, 256), BF16),
            pltpu.VMEM((2, 3, 64, 256), BF16),
            pltpu.VMEM((2, 3, 128, 256), BF16),
            pltpu.SemaphoreType.DMA((N_SEND,)),
            pltpu.SemaphoreType.DMA((N_RECV,)),
            pltpu.SemaphoreType.DMA((5,)),
        ],
        compiler_params=pltpu.CompilerParams(
            collective_id=0, has_side_effects=True, vmem_limit_bytes=60 * 2**20
        ),
        name="mixer_backward",
    )(inputs, projections, upstream_grad, jnp.asarray(cosine), jnp.asarray(sine))


def solution(mesh):
    return jax.shard_map(
        shards,
        mesh=mesh,
        in_specs=(P(("dp", "tensor"), None), P(None, "dp", "tensor"), P("dp", "tensor")),
        out_specs=(P(("dp", "tensor"), None), P(None, "dp", "tensor")),
        check_vma=False,
    )
```

```python
import functools

import jax
import jax.numpy as jnp
import numpy as np
from jax import lax
from jax.experimental import pallas as pl
from jax.experimental.pallas import tpu as pltpu
from jax.sharding import PartitionSpec as P

HS = 128
SEQ = 640
D = 4096
MESH = pl.DeviceIdType.MESH
F32 = jnp.float32
BF16 = jnp.bfloat16
HALF = D // 2
MIDDLE = pl.ds(1536, 1024)
W_PAIRS = (
    ((2, 2), (2, 1)), ((1, 2), (-1, 2)), ((2, -1), (2, 0)), ((1, 1), (-1, 1)),
    ((1, -1), (-1, -1)), ((0, 2), (0, 1)), ((1, 0), (-1, 0)), ((0, -1), (0, 0)),
)
POSITION = {2: 0, 1: 1, -1: 2, 0: 3}


def rotary_tables():
    half = HS // 2
    frequency = 10000.0 ** (-np.arange(half, dtype=np.float64) / half)
    angles = np.arange(SEQ, dtype=np.float64)[:, None] * frequency[None, :]
    cosine, sine = np.cos(angles), np.sin(angles)
    return (
        np.concatenate([cosine, cosine], -1).astype(np.float32),
        np.concatenate([-sine, sine], -1).astype(np.float32),
    )


def dot_nn(a, b):
    return lax.dot_general(a, b, (((1,), (0,)), ((), ())), preferred_element_type=F32)


def dot_nt(a, b):
    return lax.dot_general(a, b, (((1,), (1,)), ((), ())), preferred_element_type=F32)


def dot_tn(a, b):
    return lax.dot_general(a, b, (((0,), (0,)), ((), ())), preferred_element_type=F32)


N_SEND = 128
N_RECV = 128


def kernel(
    x_in, w_in, up_in, cos_in, sin_in, dx_out, dw_out,
    xv, wv, upv, cosv, sinv, pacc, qkv, gv, gr, gt, accv, dxp, dwp,
    rel_v, fin_v, zl_v, zb_v, sib_v, xrel_v, xfin_v, zrel_v, zfin_v,
    send_sem, recv_sem, local_sem, far_sem, sib_sem,
):
    dp = lax.axis_index("dp")
    tensor = lax.axis_index("tensor")
    x, zh, c = dp // 8, (dp // 2) % 4, dp % 2
    y, zl = tensor // 2, tensor % 2

    def place(xx, zz, cc, yy, ll):
        return {"dp": xx * 8 + zz * 2 + cc, "tensor": yy * 2 + ll}

    def ring(v, step):
        return lax.rem(v + (step + 4), 4)

    yp, ym = place(x, zh, c, ring(y, 1), zl), place(x, zh, c, ring(y, -1), zl)
    xp, xm = place(ring(x, 1), zh, c, y, zl), place(ring(x, -1), zh, c, y, zl)
    zp, zm = place(x, ring(zh, 1), c, y, zl), place(x, ring(zh, -1), c, y, zl)
    mate = place(x, zh, c, y, 1 - zl)
    sibling = place(x, zh, 1 - c, y, zl)
    everyone = (yp, ym, xp, xm, zp, zm, mate, sibling)

    keys = {}
    sends = []

    def key_index(key):
        return keys.setdefault(key, len(keys))

    def send(src, dst, key, device):
        copy = pltpu.make_async_remote_copy(
            src_ref=src, dst_ref=dst, send_sem=send_sem.at[len(sends)],
            recv_sem=recv_sem.at[key_index(key)], device_id=device, device_id_type=MESH,
        )
        copy.start()
        sends.append(copy)

    def recv(dst, key, device):
        pltpu.make_async_remote_copy(
            src_ref=dst, dst_ref=dst, send_sem=send_sem.at[0],
            recv_sem=recv_sem.at[key_index(key)], device_id=device, device_id_type=MESH,
        ).wait_recv()

    def rows(yy, ll):
        return pl.ds(pl.multiple_of(yy * 160 + ll * 80, 16), 80)

    def cols(h):
        return pl.ds(h * HALF, HALF)

    def slot(dy, dz):
        return pl.ds(160 * POSITION[dy] + 80 * dz, 80)

    own_x = xv.at[slot(0, 0)]

    def unit(xx, zz):
        return wv.at[:, xx * 4 + zz, c]

    locals_ = [
        pltpu.make_async_copy(x_in, own_x, local_sem.at[0]),
        pltpu.make_async_copy(w_in, unit(x, zh), local_sem.at[1]),
        pltpu.make_async_copy(up_in, upv, local_sem.at[2]),
        pltpu.make_async_copy(cos_in, cosv, local_sem.at[3]),
        pltpu.make_async_copy(sin_in, sinv, local_sem.at[4]),
    ]
    for copy in locals_:
        copy.start()

    barrier = pltpu.get_barrier_semaphore()
    for device in everyone:
        pl.semaphore_signal(barrier, inc=1, device_id=device, device_id_type=MESH)
    pl.semaphore_wait(barrier, len(everyone))

    top, bottom = pl.ds(0, 64), pl.ds(64, 64)

    def unit_half(xx, zz, part):
        return wv.at[:, xx * 4 + zz, c, part]

    def group(xx, cc):
        return wv.at[:, pl.ds(xx * 4, 4), cc]

    xn, xq, x2 = ring(x, -1), ring(x, 1), ring(x, 2)
    zn, zq, z2 = ring(zh, -1), ring(zh, 1), ring(zh, 2)

    def quarter(k):
        return pl.ds((0, 768, 2560, 3328)[k], 768)

    def xpiece(dy, dz, part):
        return xv.at[slot(dy, dz), part]

    def to_mate(k):
        send(x_in.at[:, quarter(k)], xpiece(0, 1, quarter(k)), ("Xp", k), mate)

    to_mate(0)
    to_mate(2)
    send(w_in, unit(x, zh), ("W", 0, -1), zp)
    send(w_in, unit(x, zh), ("W", 0, 1), zm)
    for h in range(2):
        send(x_in.at[:, cols(h)], xpiece(-1, 0, cols(h)), ("Xo", -1, h), yp)
        send(x_in.at[:, cols(1 - h)], xpiece(1, 0, cols(1 - h)), ("Xo", 1, 1 - h), ym)
    send(w_in, unit(x, zh), ("W", -1, 0), xp)
    send(w_in, unit(x, zh), ("W", 1, 0), xm)
    for copy in locals_:
        copy.wait()

    def pass_on(piece, key, device):
        send(piece, piece, key, device)

    def mate_piece(k):
        piece = xpiece(0, 1, quarter(k))
        recv(piece, ("Xp", k), mate)
        send(piece, xpiece(-1, 1, quarter(k)), ("Xq", -1, k), yp)
        send(piece, xpiece(1, 1, quarter(k)), ("Xq", 1, k), ym)

    def far_piece(k):
        dy, source, device = (-1, ym, yp) if k < 2 else (1, yp, ym)
        piece = xpiece(dy, 1, quarter(k))
        recv(piece, ("Xq", dy, k), source)
        send(piece, xpiece(2, 1, quarter(k)), ("Xr", 1, k), device)

    recv(unit(xn, zh), ("W", -1, 0), xm)
    pass_on(unit(xn, zh), ("W", 2, 0), xp)
    recv(unit(xq, zh), ("W", 1, 0), xp)

    mate_piece(0)
    mate_piece(2)
    to_mate(1)
    to_mate(3)
    recv(unit(x, zn), ("W", 0, -1), zm)
    pass_on(unit_half(x, zn, top), "WrA", zp)
    pass_on(unit(x, zn), ("W", -1, -1), xp)
    pass_on(unit(x, zn), ("W", 1, -1), xm)
    recv(unit(x, zq), ("W", 0, 1), zp)
    pass_on(unit_half(x, zq, bottom), "WrB", zm)
    pass_on(unit(x, zq), ("W", -1, 1), xp)
    pass_on(unit(x, zq), ("W", 1, 1), xm)

    recv(xpiece(-1, 0, cols(0)), ("Xo", -1, 0), ym)
    send(xpiece(-1, 0, cols(0)), xpiece(2, 0, cols(0)), ("Xr", 0, 0), yp)
    recv(xpiece(1, 0, cols(1)), ("Xo", 1, 1), yp)
    send(xpiece(1, 0, cols(1)), xpiece(2, 0, cols(1)), ("Xr", 0, 1), ym)

    def middle_piece(dy):
        send(xpiece(dy, 0, MIDDLE), xpiece(dy, 1, MIDDLE), ("Xb", dy), mate)


    recv(unit_half(x, z2, top), "WrA", zm)
    recv(unit_half(x, z2, bottom), "WrB", zp)
    pass_on(unit(x, z2), ("W", -1, 2), xp)
    pass_on(unit(x, z2), ("W", 1, 2), xm)
    pass_on(group(x, c), ("S", 0), sibling)
    mate_piece(1)
    mate_piece(3)
    middle_piece(0)
    recv(xpiece(-1, 0, cols(1)), ("Xo", -1, 1), ym)
    middle_piece(-1)
    recv(xpiece(1, 0, cols(0)), ("Xo", 1, 0), yp)
    middle_piece(1)

    recv(unit(xn, zn), ("W", -1, -1), xm)
    pass_on(unit(xn, zn), ("W", 2, -1), xp)
    recv(unit(xq, zq), ("W", 1, 1), xp)
    pass_on(unit(xq, zq), ("W", 2, 1), xm)
    far_piece(0)
    far_piece(2)
    recv(unit(xq, zn), ("W", 1, -1), xp)
    recv(unit(xn, zq), ("W", -1, 1), xm)
    recv(unit(xq, z2), ("W", 1, 2), xp)
    pass_on(unit(xq, z2), ("W", 2, 2), xm)
    recv(unit(xn, z2), ("W", -1, 2), xm)
    pass_on(group(xn, c), ("S", -1), sibling)
    pass_on(group(xq, c), ("S", 1), sibling)
    far_piece(1)
    far_piece(3)

    recv(xpiece(2, 0, cols(0)), ("Xr", 0, 0), ym)
    recv(xpiece(2, 0, cols(1)), ("Xr", 0, 1), yp)
    middle_piece(2)
    for dy in (0, -1, 1):
        recv(xpiece(dy, 1, MIDDLE), ("Xb", dy), mate)
    for k in (2, 3):
        recv(xpiece(-1, 1, quarter(k)), ("Xq", -1, k), ym)
    for k in (0, 1):
        recv(xpiece(1, 1, quarter(k)), ("Xq", 1, k), yp)
    near_rows = pl.ds(160, 480)

    def project_group(xx, first):
        @pl.loop(0, 3)
        def _(j):
            t = dot_nn(
                xv[near_rows, pl.ds(pl.multiple_of(xx * 1024, 1024), 1024)],
                wv[j, pl.ds(xx * 4, 4)].reshape(1024, 256),
            )
            if first:
                pacc[j, near_rows] = t
            else:
                pacc[j, near_rows] += t

    recv(group(x, 1 - c), ("S", 0), sibling)
    project_group(x, True)
    recv(group(xn, 1 - c), ("S", -1), sibling)
    project_group(xn, False)
    recv(unit(x2, zh), ("W", 2, 0), xm)
    recv(unit(x2, zn), ("W", 2, -1), xm)
    recv(unit(x2, zq), ("W", 2, 1), xp)
    recv(unit(x2, z2), ("W", 2, 2), xp)
    pass_on(group(x2, c), ("S", 2), sibling)
    recv(group(xq, 1 - c), ("S", 1), sibling)
    project_group(xq, False)
    recv(group(x2, 1 - c), ("S", 2), sibling)
    project_group(x2, False)

    def place_rows(j, dy, dz, p):
        r = rows(ring(y, dy), zl if dz == 0 else 1 - zl)
        rotated = j < 2
        cc = jnp.where(rotated, cosv[r], 1.0)
        ss = jnp.where(rotated, sinv[r], 0.0)
        for h in range(2):
            ph = p[:, h * HS:(h + 1) * HS]
            qkv[j, h, r] = (ph * cc + pltpu.roll(ph, 64, 1) * ss).astype(BF16)

    @pl.loop(0, 3)
    def _(j):
        for dy in (1, -1, 0):
            for dz in range(2):
                place_rows(j, dy, dz, pacc[j, slot(dy, dz)])

    recv(xpiece(2, 1, MIDDLE), ("Xb", 2), mate)
    for k in (0, 1):
        recv(xpiece(2, 1, quarter(k)), ("Xr", 1, k), ym)
    for k in (2, 3):
        recv(xpiece(2, 1, quarter(k)), ("Xr", 1, k), yp)

    @pl.loop(0, 3)
    def _(j):
        p = dot_nn(xv[pl.ds(0, 160)], wv[j].reshape(D, 256))
        for dz in range(2):
            place_rows(j, 2, dz, p[dz * 80:(dz + 1) * 80])

    scale = HS ** -0.5
    lower = lax.broadcasted_iota(jnp.int32, (128, 128), 0) >= lax.broadcasted_iota(
        jnp.int32, (128, 128), 1
    )

    def rotate_back(v, r):
        return (v * cosv[r] - pltpu.roll(v, 64, 1) * sinv[r]).astype(BF16)

    heads = range(2)
    for i in reversed(range(5)):
        n = (i + 1) * 128
        r, head = pl.ds(i * 128, 128), pl.ds(0, n)
        q = [qkv[0, h, r] for h in heads]
        k = [qkv[1, h, head] for h in heads]
        v = [qkv[2, h, head] for h in heads]
        up = [upv[r, pl.ds(h * HS, HS)] for h in heads]
        s = [dot_nt(q[h], k[h]) for h in heads]
        gp = [dot_nt(up[h], v[h]) for h in heads]
        low, gs = [], []
        for h in heads:
            diagonal = jnp.where(lower, s[h][:, i * 128:], -1e30)
            if i:
                diagonal = jnp.concatenate([s[h][:, : i * 128], diagonal], 1)
            top_score = jnp.max(diagonal, 1, keepdims=True)
            e = jnp.exp2((diagonal - top_score) * (scale * np.log2(np.e)))
            prob = e * (1.0 / jnp.sum(e, 1, keepdims=True))
            low.append(prob.astype(BF16))
            dots = jnp.sum(low[h].astype(F32) * gp[h], 1, keepdims=True)
            gs.append((prob * (gp[h] - dots)).astype(BF16))
        for h in heads:
            gv[r, pl.ds(h * HS, HS)] = rotate_back(dot_nn(gs[h], k[h]) * scale, r)
            dk, dv = dot_tn(gs[h], q[h]), dot_tn(low[h], up[h])
            if i == 4:
                accv[h], accv[2 + h] = dk, dv
            else:
                accv[h, head] += dk
                accv[2 + h, head] += dv
    full = pl.ds(0, SEQ)
    for h in heads:
        gv[:, pl.ds(256 + h * HS, HS)] = rotate_back(accv[h] * scale, full)
        gv[:, pl.ds(512 + h * HS, HS)] = accv[2 + h].astype(BF16)
    for dy in POSITION:
        for dz in range(2):
            gr[slot(dy, dz)] = gv[rows(ring(y, dy), zl if dz == 0 else 1 - zl)]

    zs = {0: zh, 1: zq, 2: z2, -1: zn}

    def x_term(i):
        total = None
        for j in range(3):
            w = wv[j, pl.ds(i * 2, 2)].reshape(512, 256)
            t = dot_nt(gr[:, j * 256:(j + 1) * 256], w)
            total = t if total is None else total + t
        dxp[:, pl.ds(pl.multiple_of(i * 512, 512), 512)] = total.astype(BF16)

    far_key = len(keys)
    for p in range(3):
        for h in range(2):
            key_index(("R", 1, p, h))
    sibling_key = len(keys)
    for pair in W_PAIRS:
        for dx, dz in pair:
            key_index(("DS", dx, dz))

    def w_terms(n):
        (dx0, dz0), (dx1, dz1) = W_PAIRS[n]
        b0 = ring(x, dx0) * 4 + zs[dz0]
        b1 = ring(x, dx1) * 4 + zs[dz1]

        @pl.loop(0, 2)
        def _(step):
            b = b0 + step * (b1 - b0)
            t = dot_nn(gt[...], xv[:, pl.ds(pl.multiple_of(b * 256, 256), 256)])
            for cc in range(2):
                for j in range(3):
                    dwp[b, cc, j] = t[j * 256:(j + 1) * 256, cc * 128:(cc + 1) * 128].astype(BF16)
            pltpu.make_async_remote_copy(
                src_ref=dwp.at[b, 1 - c], dst_ref=sib_v.at[b],
                send_sem=sib_sem.at[n, step], recv_sem=recv_sem.at[sibling_key + 2 * n + step],
                device_id=sibling, device_id_type=MESH,
            ).start()

    def w_sibling(dx, dz):
        b = ring(x, dx) * 4 + zs[dz]
        recv(sib_v.at[b], ("DS", dx, dz), sibling)
        add_into(dwp.at[b, c], sib_v.at[b])

    def add_rows(dst, *parts):
        rows_, step = dst.shape[0], 16 if len(dst.shape) == 2 else 1

        @pl.loop(0, rows_ // step)
        def _(i):
            r = pl.ds(pl.multiple_of(i * step, step), step)
            total = dst[r].astype(F32)
            for part in parts:
                total = total + part[r].astype(F32)
            dst[r] = total.astype(BF16)

    def add_into(dst, src):
        add_rows(dst, src)

    def add_two(dst, one, two):
        add_rows(dst, one, two)

    def xpart(dy, dz, part):
        return dxp.at[slot(dy, dz), part]

    def wunit(xx, zz):
        return dwp.at[xx * 4 + zz, c]

    def side(h, part):
        return pl.ds((1536, 2048)[h], 512) if part == 2 else pl.ds((0, 2560)[h], 1536)

    def piece(dy, part, h):
        return xpart(dy, part % 2, side(h, part))

    def arrivals(ref, part, *index):
        return ref.at[(*index, part, slice(None), pl.ds(0, 512 if part == 2 else 1536))]

    def far_own(part):
        for h in range(2):
            send(piece(2, part, h), arrivals(rel_v, part, h), ("R", h, part), (yp, ym)[h])

    def near_x(s, part, h):
        dy, device = ((1, yp), (-1, ym))[s]
        send(piece(dy, part, h), arrivals(fin_v, part, s, h), ("F", s, part, h), device)

    def near_both(part):
        near_x(0, part, 1)
        near_x(1, part, 0)

    def relay_x(part, h):
        dy, source = ((1, ym), (-1, yp))[h]
        if part == 1:
            for p in range(3):
                recv(rel_v.at[h, 1, :, pl.ds(512 * p, 512)], ("R", 1, p, h), source)
        else:
            recv(arrivals(rel_v, part, h), ("R", h, part), source)
        add_into(piece(dy, part, h), arrivals(rel_v, part, h))
        near_x(h, part, h)

    def x_middle():
        @pl.loop(3, 5)
        def _(i):
            x_term(i)

        for dy in POSITION:
            middle_x(dy)

    def x_outer():
        @pl.loop(0, 3)
        def _(p):
            for h in range(2):
                x_term(p + 5 * h)
                first = pl.multiple_of((p + 5 * h) * 512, 512)
                pltpu.make_async_remote_copy(
                    src_ref=xpart(2, 1, pl.ds(first, 512)),
                    dst_ref=rel_v.at[h, 1, :, pl.ds(pl.multiple_of(p * 512, 512), 512)],
                    send_sem=far_sem.at[p, h], recv_sem=recv_sem.at[far_key + 2 * p + h],
                    device_id=(yp, ym)[h], device_id_type=MESH,
                ).start()

    def middle_x(dy):
        send(xpart(dy, 1, MIDDLE), zb_v.at[POSITION[dy]], ("ZB", dy), mate)

    def add_middle(dy):
        recv(zb_v.at[POSITION[dy]], ("ZB", dy), mate)
        add_into(xpart(dy, 0, MIDDLE), zb_v.at[POSITION[dy]])

    def recv_near(s, part, h):
        recv(arrivals(fin_v, part, s, h), ("F", s, part, h), (ym, yp)[s])

    def own_total(part, h):
        return (
            piece(0, part, h)[...].astype(F32)
            + arrivals(fin_v, part, 0, h)[...].astype(F32)
            + arrivals(fin_v, part, 1, h)[...].astype(F32)
        )

    up_units = (2, -1)
    def far_w(dz):
        if dz in up_units:
            send(wunit(x2, zs[dz]), xrel_v.at[zs[dz]], ("XR", dz), xp)
        else:
            send(wunit(x2, zs[dz]), xrel_v.at[zs[dz]], ("XR", dz), xm)

    def relay_w(dz):
        if dz in up_units:
            recv(xrel_v.at[zs[dz]], ("XR", dz), xm)
            add_into(wunit(xq, zs[dz]), xrel_v.at[zs[dz]])
        else:
            recv(xrel_v.at[zs[dz]], ("XR", dz), xp)
            add_into(wunit(xn, zs[dz]), xrel_v.at[zs[dz]])

    def near_w(dz):
        relay_w(dz)
        send(wunit(xq, zs[dz]), xfin_v.at[0, zs[dz]], ("XF", 0, dz), xp)
        send(wunit(xn, zs[dz]), xfin_v.at[1, zs[dz]], ("XF", 1, dz), xm)

    def sum_w(dz):
        recv(xfin_v.at[0, zs[dz]], ("XF", 0, dz), xm)
        recv(xfin_v.at[1, zs[dz]], ("XF", 1, dz), xp)
        add_two(wunit(x, zs[dz]), xfin_v.at[0, zs[dz]], xfin_v.at[1, zs[dz]])

    top, bottom = pl.ds(0, 128), pl.ds(128, 128)

    def wz_half(zz, part):
        return dwp.at[x * 4 + zz, c, :, part]

    def mate_x(h):
        recv_near(0, 1, h)
        recv_near(1, 1, h)
        add_rows(piece(0, 1, h), arrivals(fin_v, 1, 0, h), arrivals(fin_v, 1, 1, h))
        send(piece(0, 1, h), zl_v.at[h], ("Z", h), mate)

    def z_far():
        send(wz_half(z2, top), zrel_v.at[0], ("ZR", 0), zp)
        send(wz_half(z2, bottom), zrel_v.at[1], ("ZR", 1), zm)

    def z_near(s, part, k):
        zz, device = ((zq, zp), (zn, zm))[s]
        send(wz_half(zz, part), zfin_v.at[s, :, part], ("ZF", s, k), device)

    def z_relay(s):
        zz, part, source = ((zq, top, zm), (zn, bottom, zp))[s]
        recv(zrel_v.at[s], ("ZR", s), source)
        add_into(wz_half(zz, part), zrel_v.at[s])
        z_near(s, part, s)

    def finish_x(h):
        recv(zl_v.at[h], ("Z", h), mate)
        recv_near(0, 0, h)
        recv_near(1, 0, h)
        dx_out[:, side(h, 0)] = (own_total(0, h) + zl_v[h].astype(F32)).astype(BF16)

    def finish_middle(h):
        recv_near(0, 2, h)
        recv_near(1, 2, h)
        dx_out[:, side(h, 2)] = own_total(2, h).astype(BF16)

    def finish_w():
        recv(zfin_v.at[0, :, bottom], ("ZF", 0, 1), zm)
        recv(zfin_v.at[0, :, top], ("ZF", 0, 0), zm)
        recv(zfin_v.at[1, :, top], ("ZF", 1, 0), zp)
        recv(zfin_v.at[1, :, bottom], ("ZF", 1, 1), zp)
        for j in range(3):
            total = (
                dwp[x * 4 + zh, c, j].astype(F32)
                + zfin_v[0, j].astype(F32)
                + zfin_v[1, j].astype(F32)
            )
            dw_out[j] = total.T

    x_outer()
    gt[...] = gr[...].T
    near_both(1)
    x_middle()
    w_terms(4)
    w_terms(0)
    w_terms(2)
    w_sibling(2, 2)
    w_sibling(-1, -1)
    far_w(2)
    w_terms(7)
    relay_x(1, 0)
    w_terms(6)
    w_sibling(2, 1)
    far_w(1)
    w_terms(5)
    w_sibling(2, -1)
    w_sibling(0, 0)
    relay_x(1, 1)
    far_w(-1)
    w_terms(1)
    w_sibling(1, 2)
    w_sibling(-1, 2)
    w_sibling(1, -1)
    w_sibling(1, 0)
    near_w(2)
    w_terms(3)
    mate_x(0)
    far_own(0)
    w_sibling(0, 2)
    w_sibling(2, 0)
    mate_x(1)
    w_sibling(-1, 1)
    w_sibling(1, 1)
    add_middle(2)
    add_middle(-1)
    add_middle(1)
    near_w(-1)
    sum_w(2)
    far_own(2)
    near_w(1)
    relay_x(0, 1)
    near_both(2)
    w_sibling(-1, 0)
    w_sibling(0, -1)
    near_both(0)
    relay_x(2, 0)
    w_sibling(0, 1)
    relay_x(2, 1)
    far_w(0)
    z_far()
    sum_w(-1)
    sum_w(1)
    z_near(1, top, 0)
    relay_x(0, 0)
    z_near(0, bottom, 1)
    near_w(0)
    z_relay(1)
    z_relay(0)
    finish_x(1)
    add_middle(0)
    sum_w(0)
    finish_middle(1)
    finish_x(0)
    finish_middle(0)
    finish_w()

    for copy in sends:
        copy.wait_send()
    for p in range(3):
        for h in range(2):
            block = rel_v.at[h, 1, :, pl.ds(512 * p, 512)]
            pltpu.make_async_remote_copy(
                src_ref=block, dst_ref=block, send_sem=far_sem.at[p, h],
                recv_sem=recv_sem.at[far_key], device_id=yp, device_id_type=MESH,
            ).wait_send()
    for n in range(8):
        for step in range(2):
            pltpu.make_async_remote_copy(
                src_ref=sib_v.at[0], dst_ref=sib_v.at[0], send_sem=sib_sem.at[n, step],
                recv_sem=recv_sem.at[far_key], device_id=sibling, device_id_type=MESH,
            ).wait_send()
    assert len(sends) <= N_SEND and len(keys) <= N_RECV


def shards(inputs, projections, upstream_grad):
    cosine, sine = rotary_tables()
    any_spec = pl.BlockSpec(memory_space=pl.ANY)
    vmem = pl.BlockSpec(memory_space=pltpu.VMEM)
    return pl.pallas_call(
        kernel,
        out_shape=(
            jax.ShapeDtypeStruct((80, D), BF16),
            jax.ShapeDtypeStruct((3, 128, 256), F32),
        ),
        in_specs=[any_spec] * 5,
        out_specs=(vmem, vmem),
        scratch_shapes=[
            pltpu.VMEM((SEQ, D), BF16),
            pltpu.VMEM((3, 16, 2, 128, 256), BF16),
            pltpu.VMEM((SEQ, 256), BF16),
            pltpu.VMEM((SEQ, HS), F32),
            pltpu.VMEM((SEQ, HS), F32),
            pltpu.VMEM((3, SEQ, 256), F32),
            pltpu.VMEM((3, 2, SEQ, HS), BF16),
            pltpu.VMEM((SEQ, 768), BF16),
            pltpu.VMEM((SEQ, 768), BF16),
            pltpu.VMEM((768, SEQ), BF16),
            pltpu.VMEM((4, SEQ, HS), F32),
            pltpu.VMEM((SEQ, D), BF16),
            pltpu.VMEM((16, 2, 3, 256, 128), BF16),
            pltpu.VMEM((2, 3, 80, 1536), BF16),
            pltpu.VMEM((2, 2, 3, 80, 1536), BF16),
            pltpu.VMEM((2, 80, 1536), BF16),
            pltpu.VMEM((4, 80, 1024), BF16),
            pltpu.VMEM((16, 3, 256, 128), BF16),
            pltpu.VMEM((4, 3, 256, 128), BF16),
            pltpu.VMEM((2, 4, 3, 256, 128), BF16),
            pltpu.VMEM((2, 3, 128, 128), BF16),
            pltpu.VMEM((2, 3, 256, 128), BF16),
            pltpu.SemaphoreType.DMA((N_SEND,)),
            pltpu.SemaphoreType.DMA((N_RECV,)),
            pltpu.SemaphoreType.DMA((5,)),
            pltpu.SemaphoreType.DMA((3, 2)),
            pltpu.SemaphoreType.DMA((8, 2)),
        ],
        compiler_params=pltpu.CompilerParams(
            collective_id=0, has_side_effects=True, vmem_limit_bytes=60 * 2**20
        ),
        name="mixer_backward",
    )(inputs, projections, upstream_grad, jnp.asarray(cosine), jnp.asarray(sine))


def solution(mesh):
    return jax.shard_map(
        shards,
        mesh=mesh,
        in_specs=(P(("dp", "tensor"), None), P(None, "dp", "tensor"), P("dp", "tensor")),
        out_specs=(P(("dp", "tensor"), None), P(None, "dp", "tensor")),
        check_vma=False,
    )
```

```python
import functools

import jax
import jax.numpy as jnp
import numpy as np
from jax import lax
from jax.experimental import pallas as pl
from jax.experimental.pallas import tpu as pltpu
from jax.sharding import PartitionSpec as P

HS = 128
SEQ = 640
D = 4096
MESH = pl.DeviceIdType.MESH
F32 = jnp.float32
BF16 = jnp.bfloat16
HALF = D // 2
MIDDLE = pl.ds(1536, 1024)
W_PAIRS = (
    ((2, 2), (2, 1)), ((1, 2), (-1, 2)), ((2, -1), (2, 0)), ((1, 1), (-1, 1)),
    ((1, -1), (-1, -1)), ((0, 2), (0, 1)), ((1, 0), (-1, 0)), ((0, -1), (0, 0)),
)
POSITION = {2: 0, 1: 1, -1: 2, 0: 3}


def rotary_tables():
    half = HS // 2
    frequency = 10000.0 ** (-np.arange(half, dtype=np.float64) / half)
    angles = np.arange(SEQ, dtype=np.float64)[:, None] * frequency[None, :]
    cosine, sine = np.cos(angles), np.sin(angles)
    return (
        np.concatenate([cosine, cosine], -1).astype(np.float32),
        np.concatenate([-sine, sine], -1).astype(np.float32),
    )


def dot_nn(a, b):
    return lax.dot_general(a, b, (((1,), (0,)), ((), ())), preferred_element_type=F32)


def dot_nt(a, b):
    return lax.dot_general(a, b, (((1,), (1,)), ((), ())), preferred_element_type=F32)


def dot_tn(a, b):
    return lax.dot_general(a, b, (((0,), (0,)), ((), ())), preferred_element_type=F32)


N_SEND = 128
N_RECV = 128


def kernel(
    x_in, w_in, up_in, cos_in, sin_in, dx_out, dw_out,
    xv, wv, upv, cosv, sinv, pacc, qkv, gv, gr, gt, accv, dxp, dwp,
    rel_v, fin_v, zl_v, zb_v, sib_v, xrel_v, xfin_v, zrel_v, zfin_v,
    send_sem, recv_sem, local_sem, far_sem, sib_sem,
):
    dp = lax.axis_index("dp")
    tensor = lax.axis_index("tensor")
    x, zh, c = dp // 8, (dp // 2) % 4, dp % 2
    y, zl = tensor // 2, tensor % 2

    def place(xx, zz, cc, yy, ll):
        return {"dp": xx * 8 + zz * 2 + cc, "tensor": yy * 2 + ll}

    def ring(v, step):
        return lax.rem(v + (step + 4), 4)

    yp, ym = place(x, zh, c, ring(y, 1), zl), place(x, zh, c, ring(y, -1), zl)
    xp, xm = place(ring(x, 1), zh, c, y, zl), place(ring(x, -1), zh, c, y, zl)
    zp, zm = place(x, ring(zh, 1), c, y, zl), place(x, ring(zh, -1), c, y, zl)
    mate = place(x, zh, c, y, 1 - zl)
    sibling = place(x, zh, 1 - c, y, zl)
    everyone = (yp, ym, xp, xm, zp, zm, mate, sibling)

    keys = {}
    sends = []

    def key_index(key):
        return keys.setdefault(key, len(keys))

    def send(src, dst, key, device):
        copy = pltpu.make_async_remote_copy(
            src_ref=src, dst_ref=dst, send_sem=send_sem.at[len(sends)],
            recv_sem=recv_sem.at[key_index(key)], device_id=device, device_id_type=MESH,
        )
        copy.start()
        sends.append(copy)

    def recv(dst, key, device):
        pltpu.make_async_remote_copy(
            src_ref=dst, dst_ref=dst, send_sem=send_sem.at[0],
            recv_sem=recv_sem.at[key_index(key)], device_id=device, device_id_type=MESH,
        ).wait_recv()

    def rows(yy, ll):
        return pl.ds(pl.multiple_of(yy * 160 + ll * 80, 16), 80)

    def cols(h):
        return pl.ds(h * HALF, HALF)

    def slot(dy, dz):
        return pl.ds(160 * POSITION[dy] + 80 * dz, 80)

    own_x = xv.at[slot(0, 0)]

    def unit(xx, zz):
        return wv.at[:, xx * 4 + zz, c]

    locals_ = [
        pltpu.make_async_copy(x_in, own_x, local_sem.at[0]),
        pltpu.make_async_copy(w_in, unit(x, zh), local_sem.at[1]),
        pltpu.make_async_copy(up_in, upv, local_sem.at[2]),
        pltpu.make_async_copy(cos_in, cosv, local_sem.at[3]),
        pltpu.make_async_copy(sin_in, sinv, local_sem.at[4]),
    ]
    barrier = pltpu.get_barrier_semaphore()
    for device in everyone:
        pl.semaphore_signal(barrier, inc=1, device_id=device, device_id_type=MESH)
    for copy in locals_:
        copy.start()
    pl.semaphore_wait(barrier, len(everyone))

    top, bottom = pl.ds(0, 64), pl.ds(64, 64)

    def unit_half(xx, zz, part):
        return wv.at[:, xx * 4 + zz, c, part]

    def group(xx, cc):
        return wv.at[:, pl.ds(xx * 4, 4), cc]

    xn, xq, x2 = ring(x, -1), ring(x, 1), ring(x, 2)
    zn, zq, z2 = ring(zh, -1), ring(zh, 1), ring(zh, 2)

    def quarter(k):
        return pl.ds((0, 768, 2560, 3328)[k], 768)

    def xpiece(dy, dz, part):
        return xv.at[slot(dy, dz), part]

    def to_mate(k):
        send(x_in.at[:, quarter(k)], xpiece(0, 1, quarter(k)), ("Xp", k), mate)

    to_mate(0)
    to_mate(2)
    send(w_in, unit(x, zh), ("W", 0, -1), zp)
    send(w_in, unit(x, zh), ("W", 0, 1), zm)
    for h in range(2):
        send(x_in.at[:, cols(h)], xpiece(-1, 0, cols(h)), ("Xo", -1, h), yp)
        send(x_in.at[:, cols(1 - h)], xpiece(1, 0, cols(1 - h)), ("Xo", 1, 1 - h), ym)
    send(w_in, unit(x, zh), ("W", -1, 0), xp)
    send(w_in, unit(x, zh), ("W", 1, 0), xm)
    for copy in locals_:
        copy.wait()

    def pass_on(piece, key, device):
        send(piece, piece, key, device)

    def mate_piece(k):
        piece = xpiece(0, 1, quarter(k))
        recv(piece, ("Xp", k), mate)
        send(piece, xpiece(-1, 1, quarter(k)), ("Xq", -1, k), yp)
        send(piece, xpiece(1, 1, quarter(k)), ("Xq", 1, k), ym)

    def far_piece(k):
        dy, source, device = (-1, ym, yp) if k < 2 else (1, yp, ym)
        piece = xpiece(dy, 1, quarter(k))
        recv(piece, ("Xq", dy, k), source)
        send(piece, xpiece(2, 1, quarter(k)), ("Xr", 1, k), device)

    recv(unit(xn, zh), ("W", -1, 0), xm)
    pass_on(unit(xn, zh), ("W", 2, 0), xp)
    recv(unit(xq, zh), ("W", 1, 0), xp)

    mate_piece(0)
    mate_piece(2)
    to_mate(1)
    to_mate(3)
    recv(unit(x, zn), ("W", 0, -1), zm)
    pass_on(unit_half(x, zn, top), "WrA", zp)
    pass_on(unit(x, zn), ("W", -1, -1), xp)
    pass_on(unit(x, zn), ("W", 1, -1), xm)
    recv(unit(x, zq), ("W", 0, 1), zp)
    pass_on(unit_half(x, zq, bottom), "WrB", zm)
    pass_on(unit(x, zq), ("W", -1, 1), xp)
    pass_on(unit(x, zq), ("W", 1, 1), xm)

    recv(xpiece(-1, 0, cols(0)), ("Xo", -1, 0), ym)
    send(xpiece(-1, 0, cols(0)), xpiece(2, 0, cols(0)), ("Xr", 0, 0), yp)
    recv(xpiece(1, 0, cols(1)), ("Xo", 1, 1), yp)
    send(xpiece(1, 0, cols(1)), xpiece(2, 0, cols(1)), ("Xr", 0, 1), ym)

    def middle_piece(dy):
        send(xpiece(dy, 0, MIDDLE), xpiece(dy, 1, MIDDLE), ("Xb", dy), mate)


    recv(unit_half(x, z2, top), "WrA", zm)
    recv(unit_half(x, z2, bottom), "WrB", zp)
    pass_on(unit(x, z2), ("W", -1, 2), xp)
    pass_on(unit(x, z2), ("W", 1, 2), xm)
    pass_on(group(x, c), ("S", 0), sibling)
    mate_piece(1)
    mate_piece(3)
    middle_piece(0)
    recv(xpiece(-1, 0, cols(1)), ("Xo", -1, 1), ym)
    middle_piece(-1)
    recv(xpiece(1, 0, cols(0)), ("Xo", 1, 0), yp)
    middle_piece(1)

    recv(unit(xn, zn), ("W", -1, -1), xm)
    pass_on(unit(xn, zn), ("W", 2, -1), xp)
    recv(unit(xq, zq), ("W", 1, 1), xp)
    pass_on(unit(xq, zq), ("W", 2, 1), xm)
    far_piece(0)
    far_piece(2)
    recv(unit(xq, zn), ("W", 1, -1), xp)
    recv(unit(xn, zq), ("W", -1, 1), xm)
    recv(unit(xq, z2), ("W", 1, 2), xp)
    pass_on(unit(xq, z2), ("W", 2, 2), xm)
    recv(unit(xn, z2), ("W", -1, 2), xm)
    pass_on(group(xn, c), ("S", -1), sibling)
    pass_on(group(xq, c), ("S", 1), sibling)
    far_piece(1)
    far_piece(3)

    recv(xpiece(2, 0, cols(0)), ("Xr", 0, 0), ym)
    recv(xpiece(2, 0, cols(1)), ("Xr", 0, 1), yp)
    middle_piece(2)
    for dy in (0, -1, 1):
        recv(xpiece(dy, 1, MIDDLE), ("Xb", dy), mate)
    for k in (2, 3):
        recv(xpiece(-1, 1, quarter(k)), ("Xq", -1, k), ym)
    for k in (0, 1):
        recv(xpiece(1, 1, quarter(k)), ("Xq", 1, k), yp)
    near_rows = pl.ds(160, 480)

    def project_group(xx, first):
        @pl.loop(0, 3)
        def _(j):
            t = dot_nn(
                xv[near_rows, pl.ds(pl.multiple_of(xx * 1024, 1024), 1024)],
                wv[j, pl.ds(xx * 4, 4)].reshape(1024, 256),
            )
            if first:
                pacc[j, near_rows] = t
            else:
                pacc[j, near_rows] += t

    recv(group(x, 1 - c), ("S", 0), sibling)
    project_group(x, True)
    recv(group(xn, 1 - c), ("S", -1), sibling)
    project_group(xn, False)
    recv(unit(x2, zh), ("W", 2, 0), xm)
    recv(unit(x2, zn), ("W", 2, -1), xm)
    recv(unit(x2, zq), ("W", 2, 1), xp)
    recv(unit(x2, z2), ("W", 2, 2), xp)
    pass_on(group(x2, c), ("S", 2), sibling)
    recv(group(xq, 1 - c), ("S", 1), sibling)
    project_group(xq, False)
    recv(group(x2, 1 - c), ("S", 2), sibling)
    project_group(x2, False)

    def place_rows(j, dy, dz, p):
        r = rows(ring(y, dy), zl if dz == 0 else 1 - zl)
        rotated = j < 2
        cc = jnp.where(rotated, cosv[r], 1.0)
        ss = jnp.where(rotated, sinv[r], 0.0)
        for h in range(2):
            ph = p[:, h * HS:(h + 1) * HS]
            qkv[j, h, r] = (ph * cc + pltpu.roll(ph, 64, 1) * ss).astype(BF16)

    @pl.loop(0, 3)
    def _(j):
        for dy in (1, -1, 0):
            for dz in range(2):
                place_rows(j, dy, dz, pacc[j, slot(dy, dz)])

    recv(xpiece(2, 1, MIDDLE), ("Xb", 2), mate)
    for k in (0, 1):
        recv(xpiece(2, 1, quarter(k)), ("Xr", 1, k), ym)
    for k in (2, 3):
        recv(xpiece(2, 1, quarter(k)), ("Xr", 1, k), yp)

    @pl.loop(0, 3)
    def _(j):
        p = dot_nn(xv[pl.ds(0, 160)], wv[j].reshape(D, 256))
        for dz in range(2):
            place_rows(j, 2, dz, p[dz * 80:(dz + 1) * 80])

    scale = HS ** -0.5
    lower = lax.broadcasted_iota(jnp.int32, (128, 128), 0) >= lax.broadcasted_iota(
        jnp.int32, (128, 128), 1
    )

    def rotate_back(v, r):
        return (v * cosv[r] - pltpu.roll(v, 64, 1) * sinv[r]).astype(BF16)

    heads = range(2)
    for i in reversed(range(5)):
        n = (i + 1) * 128
        r, head = pl.ds(i * 128, 128), pl.ds(0, n)
        q = [qkv[0, h, r] for h in heads]
        k = [qkv[1, h, head] for h in heads]
        v = [qkv[2, h, head] for h in heads]
        up = [upv[r, pl.ds(h * HS, HS)] for h in heads]
        s = [dot_nt(q[h], k[h]) for h in heads]
        gp = [dot_nt(up[h], v[h]) for h in heads]
        low, gs = [], []
        for h in heads:
            diagonal = jnp.where(lower, s[h][:, i * 128:], -1e30)
            if i:
                diagonal = jnp.concatenate([s[h][:, : i * 128], diagonal], 1)
            top_score = jnp.max(diagonal, 1, keepdims=True)
            e = jnp.exp2((diagonal - top_score) * (scale * np.log2(np.e)))
            prob = e * (1.0 / jnp.sum(e, 1, keepdims=True))
            low.append(prob.astype(BF16))
            dots = jnp.sum(low[h].astype(F32) * gp[h], 1, keepdims=True)
            gs.append((prob * (gp[h] - dots)).astype(BF16))
        for h in heads:
            gv[r, pl.ds(h * HS, HS)] = rotate_back(dot_nn(gs[h], k[h]) * scale, r)
            dk, dv = dot_tn(gs[h], q[h]), dot_tn(low[h], up[h])
            if i == 4:
                accv[h], accv[2 + h] = dk, dv
            else:
                accv[h, head] += dk
                accv[2 + h, head] += dv
    full = pl.ds(0, SEQ)
    for h in heads:
        gv[:, pl.ds(256 + h * HS, HS)] = rotate_back(accv[h] * scale, full)
        gv[:, pl.ds(512 + h * HS, HS)] = accv[2 + h].astype(BF16)
    for dy in POSITION:
        for dz in range(2):
            gr[slot(dy, dz)] = gv[rows(ring(y, dy), zl if dz == 0 else 1 - zl)]

    zs = {0: zh, 1: zq, 2: z2, -1: zn}

    def x_term(i):
        total = None
        for j in range(3):
            w = wv[j, pl.ds(i * 2, 2)].reshape(512, 256)
            t = dot_nt(gr[:, j * 256:(j + 1) * 256], w)
            total = t if total is None else total + t
        dxp[:, pl.ds(pl.multiple_of(i * 512, 512), 512)] = total.astype(BF16)

    far_key = len(keys)
    for p in range(3):
        for h in range(2):
            key_index(("R", 1, p, h))
    sibling_key = len(keys)
    for pair in W_PAIRS:
        for dx, dz in pair:
            key_index(("DS", dx, dz))

    def w_terms(n):
        (dx0, dz0), (dx1, dz1) = W_PAIRS[n]
        b0 = ring(x, dx0) * 4 + zs[dz0]
        b1 = ring(x, dx1) * 4 + zs[dz1]

        @pl.loop(0, 2)
        def _(step):
            b = b0 + step * (b1 - b0)
            t = dot_nn(gt[...], xv[:, pl.ds(pl.multiple_of(b * 256, 256), 256)])
            for cc in range(2):
                for j in range(3):
                    dwp[b, cc, j] = t[j * 256:(j + 1) * 256, cc * 128:(cc + 1) * 128].astype(BF16)
            pltpu.make_async_remote_copy(
                src_ref=dwp.at[b, 1 - c], dst_ref=sib_v.at[b],
                send_sem=sib_sem.at[n, step], recv_sem=recv_sem.at[sibling_key + 2 * n + step],
                device_id=sibling, device_id_type=MESH,
            ).start()

    def w_sibling(dx, dz):
        b = ring(x, dx) * 4 + zs[dz]
        recv(sib_v.at[b], ("DS", dx, dz), sibling)
        add_into(dwp.at[b, c], sib_v.at[b])

    def add_rows(dst, *parts):
        rows_, step = dst.shape[0], 16 if len(dst.shape) == 2 else 1

        @pl.loop(0, rows_ // step)
        def _(i):
            r = pl.ds(pl.multiple_of(i * step, step), step)
            total = dst[r].astype(F32)
            for part in parts:
                total = total + part[r].astype(F32)
            dst[r] = total.astype(BF16)

    def add_into(dst, src):
        add_rows(dst, src)

    def add_two(dst, one, two):
        add_rows(dst, one, two)

    def xpart(dy, dz, part):
        return dxp.at[slot(dy, dz), part]

    def wunit(xx, zz):
        return dwp.at[xx * 4 + zz, c]

    def side(h, part):
        return pl.ds((1536, 2048)[h], 512) if part == 2 else pl.ds((0, 2560)[h], 1536)

    def piece(dy, part, h):
        return xpart(dy, part % 2, side(h, part))

    def arrivals(ref, part, *index):
        return ref.at[(*index, part, slice(None), pl.ds(0, 512 if part == 2 else 1536))]

    def far_own(part):
        for h in range(2):
            send(piece(2, part, h), arrivals(rel_v, part, h), ("R", h, part), (yp, ym)[h])

    def near_x(s, part, h):
        dy, device = ((1, yp), (-1, ym))[s]
        send(piece(dy, part, h), arrivals(fin_v, part, s, h), ("F", s, part, h), device)

    def near_both(part):
        near_x(0, part, 1)
        near_x(1, part, 0)

    def relay_x(part, h):
        dy, source = ((1, ym), (-1, yp))[h]
        if part == 1:
            for p in range(3):
                recv(rel_v.at[h, 1, :, pl.ds(512 * p, 512)], ("R", 1, p, h), source)
        else:
            recv(arrivals(rel_v, part, h), ("R", h, part), source)
        add_into(piece(dy, part, h), arrivals(rel_v, part, h))
        near_x(h, part, h)

    def x_middle():
        @pl.loop(3, 5)
        def _(i):
            x_term(i)

        for dy in POSITION:
            middle_x(dy)

    def x_outer():
        @pl.loop(0, 3)
        def _(p):
            for h in range(2):
                x_term(p + 5 * h)
                first = pl.multiple_of((p + 5 * h) * 512, 512)
                pltpu.make_async_remote_copy(
                    src_ref=xpart(2, 1, pl.ds(first, 512)),
                    dst_ref=rel_v.at[h, 1, :, pl.ds(pl.multiple_of(p * 512, 512), 512)],
                    send_sem=far_sem.at[p, h], recv_sem=recv_sem.at[far_key + 2 * p + h],
                    device_id=(yp, ym)[h], device_id_type=MESH,
                ).start()

    def middle_x(dy):
        send(xpart(dy, 1, MIDDLE), zb_v.at[POSITION[dy]], ("ZB", dy), mate)

    def add_middle(dy):
        recv(zb_v.at[POSITION[dy]], ("ZB", dy), mate)
        add_into(xpart(dy, 0, MIDDLE), zb_v.at[POSITION[dy]])

    def recv_near(s, part, h):
        recv(arrivals(fin_v, part, s, h), ("F", s, part, h), (ym, yp)[s])

    def own_total(part, h, r):
        return (
            piece(0, part, h)[r].astype(F32)
            + arrivals(fin_v, part, 0, h)[r].astype(F32)
            + arrivals(fin_v, part, 1, h)[r].astype(F32)
        )

    up_units = (2, -1)
    def far_w(dz):
        if dz in up_units:
            send(wunit(x2, zs[dz]), xrel_v.at[zs[dz]], ("XR", dz), xp)
        else:
            send(wunit(x2, zs[dz]), xrel_v.at[zs[dz]], ("XR", dz), xm)

    def relay_w(dz):
        if dz in up_units:
            recv(xrel_v.at[zs[dz]], ("XR", dz), xm)
            add_into(wunit(xq, zs[dz]), xrel_v.at[zs[dz]])
        else:
            recv(xrel_v.at[zs[dz]], ("XR", dz), xp)
            add_into(wunit(xn, zs[dz]), xrel_v.at[zs[dz]])

    def near_w(dz):
        relay_w(dz)
        send(wunit(xq, zs[dz]), xfin_v.at[0, zs[dz]], ("XF", 0, dz), xp)
        send(wunit(xn, zs[dz]), xfin_v.at[1, zs[dz]], ("XF", 1, dz), xm)

    def sum_w(dz):
        recv(xfin_v.at[0, zs[dz]], ("XF", 0, dz), xm)
        recv(xfin_v.at[1, zs[dz]], ("XF", 1, dz), xp)
        add_two(wunit(x, zs[dz]), xfin_v.at[0, zs[dz]], xfin_v.at[1, zs[dz]])

    top, bottom = pl.ds(0, 128), pl.ds(128, 128)

    def wz_half(zz, part):
        return dwp.at[x * 4 + zz, c, :, part]

    def mate_x(h):
        recv_near(0, 1, h)
        recv_near(1, 1, h)
        add_rows(piece(0, 1, h), arrivals(fin_v, 1, 0, h), arrivals(fin_v, 1, 1, h))
        send(piece(0, 1, h), zl_v.at[h], ("Z", h), mate)

    def z_far():
        send(wz_half(z2, top), zrel_v.at[0], ("ZR", 0), zp)
        send(wz_half(z2, bottom), zrel_v.at[1], ("ZR", 1), zm)

    def z_near(s, part, k):
        zz, device = ((zq, zp), (zn, zm))[s]
        send(wz_half(zz, part), zfin_v.at[s, :, part], ("ZF", s, k), device)

    def z_relay(s):
        zz, part, source = ((zq, top, zm), (zn, bottom, zp))[s]
        recv(zrel_v.at[s], ("ZR", s), source)
        add_into(wz_half(zz, part), zrel_v.at[s])
        z_near(s, part, s)

    def finish_x(h):
        recv(zl_v.at[h], ("Z", h), mate)
        recv_near(0, 0, h)
        recv_near(1, 0, h)

        @pl.loop(0, 5)
        def _(i):
            r = pl.ds(pl.multiple_of(i * 16, 16), 16)
            dx_out[r, side(h, 0)] = (own_total(0, h, r) + zl_v[h, r].astype(F32)).astype(BF16)

    def finish_middle(h):
        recv_near(0, 2, h)
        recv_near(1, 2, h)

        @pl.loop(0, 5)
        def _(i):
            r = pl.ds(pl.multiple_of(i * 16, 16), 16)
            dx_out[r, side(h, 2)] = own_total(2, h, r).astype(BF16)

    def finish_w():
        recv(zfin_v.at[0, :, bottom], ("ZF", 0, 1), zm)
        recv(zfin_v.at[0, :, top], ("ZF", 0, 0), zm)
        recv(zfin_v.at[1, :, top], ("ZF", 1, 0), zp)
        recv(zfin_v.at[1, :, bottom], ("ZF", 1, 1), zp)

        @pl.loop(0, 3)
        def _(j):
            total = (
                dwp[x * 4 + zh, c, j].astype(F32)
                + zfin_v[0, j].astype(F32)
                + zfin_v[1, j].astype(F32)
            )
            dw_out[j] = total.T

    x_outer()
    gt[...] = gr[...].T
    near_both(1)
    x_middle()
    w_terms(4)
    w_terms(0)
    w_terms(2)
    w_sibling(2, 2)
    w_sibling(-1, -1)
    far_w(2)
    w_terms(7)
    relay_x(1, 0)
    w_terms(6)
    w_sibling(2, 1)
    far_w(1)
    w_terms(5)
    w_sibling(2, -1)
    w_sibling(0, 0)
    relay_x(1, 1)
    far_w(-1)
    w_terms(1)
    w_sibling(1, 2)
    w_sibling(-1, 2)
    w_sibling(1, -1)
    w_sibling(1, 0)
    near_w(2)
    w_terms(3)
    mate_x(0)
    far_own(0)
    w_sibling(0, 2)
    w_sibling(2, 0)
    mate_x(1)
    w_sibling(-1, 1)
    w_sibling(1, 1)
    add_middle(2)
    add_middle(-1)
    add_middle(1)
    near_w(-1)
    sum_w(2)
    far_own(2)
    near_w(1)
    relay_x(0, 1)
    near_both(2)
    w_sibling(-1, 0)
    w_sibling(0, -1)
    near_both(0)
    relay_x(2, 0)
    w_sibling(0, 1)
    relay_x(2, 1)
    far_w(0)
    z_far()
    sum_w(-1)
    sum_w(1)
    z_near(1, top, 0)
    relay_x(0, 0)
    z_near(0, bottom, 1)
    near_w(0)
    z_relay(1)
    z_relay(0)
    finish_x(1)
    add_middle(0)
    sum_w(0)
    finish_middle(1)
    finish_x(0)
    finish_middle(0)
    finish_w()

    for copy in sends:
        copy.wait_send()
    for p in range(3):
        for h in range(2):
            block = rel_v.at[h, 1, :, pl.ds(512 * p, 512)]
            pltpu.make_async_remote_copy(
                src_ref=block, dst_ref=block, send_sem=far_sem.at[p, h],
                recv_sem=recv_sem.at[far_key], device_id=yp, device_id_type=MESH,
            ).wait_send()
    for n in range(8):
        for step in range(2):
            pltpu.make_async_remote_copy(
                src_ref=sib_v.at[0], dst_ref=sib_v.at[0], send_sem=sib_sem.at[n, step],
                recv_sem=recv_sem.at[far_key], device_id=sibling, device_id_type=MESH,
            ).wait_send()
    assert len(sends) <= N_SEND and len(keys) <= N_RECV


def shards(inputs, projections, upstream_grad):
    cosine, sine = rotary_tables()
    any_spec = pl.BlockSpec(memory_space=pl.ANY)
    vmem = pl.BlockSpec(memory_space=pltpu.VMEM)
    return pl.pallas_call(
        kernel,
        out_shape=(
            jax.ShapeDtypeStruct((80, D), BF16),
            jax.ShapeDtypeStruct((3, 128, 256), F32),
        ),
        in_specs=[any_spec] * 5,
        out_specs=(vmem, vmem),
        scratch_shapes=[
            pltpu.VMEM((SEQ, D), BF16),
            pltpu.VMEM((3, 16, 2, 128, 256), BF16),
            pltpu.VMEM((SEQ, 256), BF16),
            pltpu.VMEM((SEQ, HS), F32),
            pltpu.VMEM((SEQ, HS), F32),
            pltpu.VMEM((3, SEQ, 256), F32),
            pltpu.VMEM((3, 2, SEQ, HS), BF16),
            pltpu.VMEM((SEQ, 768), BF16),
            pltpu.VMEM((SEQ, 768), BF16),
            pltpu.VMEM((768, SEQ), BF16),
            pltpu.VMEM((4, SEQ, HS), F32),
            pltpu.VMEM((SEQ, D), BF16),
            pltpu.VMEM((16, 2, 3, 256, 128), BF16),
            pltpu.VMEM((2, 3, 80, 1536), BF16),
            pltpu.VMEM((2, 2, 3, 80, 1536), BF16),
            pltpu.VMEM((2, 80, 1536), BF16),
            pltpu.VMEM((4, 80, 1024), BF16),
            pltpu.VMEM((16, 3, 256, 128), BF16),
            pltpu.VMEM((4, 3, 256, 128), BF16),
            pltpu.VMEM((2, 4, 3, 256, 128), BF16),
            pltpu.VMEM((2, 3, 128, 128), BF16),
            pltpu.VMEM((2, 3, 256, 128), BF16),
            pltpu.SemaphoreType.DMA((N_SEND,)),
            pltpu.SemaphoreType.DMA((N_RECV,)),
            pltpu.SemaphoreType.DMA((5,)),
            pltpu.SemaphoreType.DMA((3, 2)),
            pltpu.SemaphoreType.DMA((8, 2)),
        ],
        compiler_params=pltpu.CompilerParams(
            collective_id=0, has_side_effects=True, vmem_limit_bytes=60 * 2**20
        ),
        name="mixer_backward",
    )(inputs, projections, upstream_grad, jnp.asarray(cosine), jnp.asarray(sine))


def solution(mesh):
    return jax.shard_map(
        shards,
        mesh=mesh,
        in_specs=(P(("dp", "tensor"), None), P(None, "dp", "tensor"), P("dp", "tensor")),
        out_specs=(P(("dp", "tensor"), None), P(None, "dp", "tensor")),
        check_vma=False,
    )
```
